256 devices in a mesh: ep: 64 (over z, y, core), tp: 4 (over x).
Axes of the slice: x: 4, y: 4, z: 8, core: 2. Of those that a mesh axis runs over, the one named last changes fastest.
Arguments:
- hidden_in: bfloat16 [8192, 3584], P('ep', 'tp'), may hold values from -16 to 16
- next_embed: bfloat16 [8192, 3584], P('ep', 'tp'), may hold values from -16 to 16
- expert_rows: bfloat16 [256, 64, 8, 3584], P('ep', None, None, 'tp'), may hold values from -6 to 6
- routes: int32 [8192, 8], P('ep'), may hold values from 0 to 255, all different within a row; in each aligned block of 128 rows (0 to 127, 128 to 255, ...) at most 8 rows name the same one
- gates: float32 [8192, 8], P('ep'), may hold values from 0.05 to 0.5
- gain_hidden: float32 [3584], P('tp'), may hold values from 0.5 to 1.5
- gain_embed: float32 [3584], P('tp'), may hold values from 0.5 to 1.5
- join_hidden: bfloat16 [3584, 3584], P('ep', 'tp'), may hold values from -0.3307189 to 0.3307189
- join_embed: bfloat16 [3584, 3584], P('ep', 'tp'), may hold values from -0.165359457 to 0.165359457
- gain_block: float32 [3584], P('tp'), may hold values from 0.5 to 1.5
- down_weight: bfloat16 [3584, 1056], P(('tp', 'ep')), may hold values from -0.09375 to 0.09375
- gain_query: float32 [768], replicated, may hold values from 0.5 to 1.5
- gain_latent: float32 [256], replicated, may hold values from 0.5 to 1.5
- query_up: bfloat16 [768, 6144], P('ep', 'tp'), may hold values from -0.5051815 to 0.5051815
- latent_up: bfloat16 [256, 8192], P('ep', 'tp'), may hold values from -0.875 to 0.875
Outputs:
- joined: bfloat16 [8192, 3584], P('ep', 'tp')
- attended: bfloat16 [8192, 4096], P('ep', 'tp')
The draws below stay inside these ranges and needn't reach their ends.
Inputs may be any that keep to these rules, and one draw needn't show every extreme that they name: `routes`: in the 128 rows of one index of ep no expert is named more than 8 times, a bound that some block reaches.
All inputs are finite; a program needn't handle non-finite values.
Results may differ from the reference program's by a relative error of at most 0.035.
Values may be sent and summed in bfloat16 or wider, within the bound.
No kernel may reach another device: no remote copies, remote signals or barrier semaphores. Data moves between devices by JAX's collectives and lax.ppermute only.
A program may use at most 128 MiB of HBM per device.

```python
import math
import jax
import jax.numpy as jnp
import numpy as np
from jax import lax

D = 3584
H = 64
NOPE = 64
ROPE = 32
VDIM = 64
QL = 768
KL = 256
TOP = 8
SEQS = 1
TOK_DEV = 128
EXPERTS = 256
TOKENS = 8192
SEQ_LEN = 8192
CAP = 8
N_EP = 64


def column_scales(key, base):
    position = jnp.arange(D, dtype=jnp.float32) / D
    spread = jax.random.uniform(jax.random.fold_in(key, 101), (D,), jnp.float32)
    return jnp.sqrt(base ** (position - 0.5) * 10.0 ** (spread - 0.5))


def rising_scales(start, ratio):
    position = jnp.arange(D, dtype=jnp.float32) / D
    return start * ratio ** position


def stream_values(own):
    values = jax.random.truncated_normal(own, -4.0, 4.0, (TOKENS, D), jnp.float32) * rising_scales(0.5, 8.0)[None, :]
    return values.astype(jnp.bfloat16)


def draw_hidden_in(key, part):
    own = jax.random.fold_in(key, 11)
    return stream_values(own)


def draw_next_embed(key, part):
    own = jax.random.fold_in(key, 13)
    return stream_values(own)


def draw_join_hidden(key, part):
    own = jax.random.fold_in(key, 3)
    scales = column_scales(key, 5.0)
    values = jax.random.truncated_normal(own, -4.0, 4.0, (D, D), jnp.float32) * scales[None, :]
    return (values * (2.0 * D) ** (-0.5)).astype(jnp.bfloat16)


def draw_join_embed(key, part):
    own = jax.random.fold_in(key, 5)
    scales = column_scales(key, 5.0)
    values = jax.random.truncated_normal(own, -4.0, 4.0, (D, D), jnp.float32) * scales[None, :]
    return (values * (2.0 * D) ** (-0.5)).astype(jnp.bfloat16)


def draw_query_up(key, part):
    own = jax.random.fold_in(key, 7)
    width = NOPE + ROPE
    values = jax.random.truncated_normal(own, -4.0, 4.0, (QL, H * width), jnp.float32)
    return (values * QL ** (-0.5)).astype(jnp.bfloat16)


def draw_latent_up(key, part):
    own = jax.random.fold_in(key, 9)
    width = NOPE + VDIM
    values = jax.random.truncated_normal(own, -4.0, 4.0, (KL, H * width), jnp.float32)
    return (values * KL ** (-0.5)).astype(jnp.bfloat16)


def steps_of(rng, extent, cuts, smallest, high):
    def one(dim, blocks):
        draws = jax.random.uniform(jax.random.fold_in(jax.random.fold_in(rng, 6), dim), (blocks,), jnp.float32, smallest / len(cuts), high / len(cuts))
        return jnp.repeat(jnp.exp(draws), extent[dim] // blocks).reshape((-1,) + (1,) * (len(extent) - dim - 1))

    level = one(*cuts[0])
    for cut in cuts[1:]:
        level = level * one(*cut)
    return level


def shared_out(key, own, number, rows, number_of, top, limit, skew):
    order = jax.random.permutation(key, number_of)
    heavy_load, usual = portions_of(number_of, rows * top, limit, skew, True), portions_of(number_of, rows * top, limit, skew, False)
    places = jnp.arange(number_of)

    def named(tallies, rotation):
        used = int((tallies > 0).sum())
        fixed = max(1, used // 4)
        passed = fixed + (places - fixed + rotation * (used - fixed)) % max(1, number_of - fixed)
        return jnp.zeros((number_of,), jnp.int32).at[order[jnp.where(places < fixed, places, passed)]].set(jnp.asarray(tallies, jnp.int32))

    tallies = jnp.where(number % 4 == 0, named(heavy_load, number // 4), named(usual, number - number // 4 - 1))
    mixed = jax.random.permutation(jax.random.fold_in(own, 3), number_of)
    donor, taker = mixed[0:number_of // 2 * 2:2], mixed[1:number_of // 2 * 2:2]
    margin = jnp.minimum(tallies[donor] - 1, limit - tallies[taker]) // 2
    margin = jnp.where((donor == order[0]) | (taker == order[0]) | (tallies[taker] == 0), 0, jnp.maximum(margin, 0))
    passed = jax.random.randint(jax.random.fold_in(own, 4), (number_of // 2,), 0, 1 << 20) % (margin + 1)
    tallies = tallies.at[donor].add(-passed).at[taker].add(passed)
    items = jnp.searchsorted(jnp.cumsum(tallies), jnp.arange(rows * top), side="right").astype(jnp.int32)
    grid = items.reshape(top, rows).T
    grid = grid[jax.random.permutation(jax.random.fold_in(own, 1), rows)]
    rotation = jax.random.randint(jax.random.fold_in(own, 2), (rows, 1), 0, top)
    return jnp.take_along_axis(grid, (jnp.arange(top)[None, :] + rotation) % top, axis=1)


def portions_of(count, total, most, slope, full):
    portions = [(1 << 20) // math.isqrt(standing ** slope) + 1 for standing in range(1, count + 1)]
    largest = most if full else min(most, max(-(-total // count), total * portions[0] // sum(portions)))
    least = 1 if total - largest >= count - 1 else 0
    holding, surplus = [largest] + [least] * (count - 1), total - largest - least * (count - 1)
    while surplus > 0:
        candidates = [i for i in range(1, count) if holding[i] < largest] or [i for i in range(1, count) if holding[i] < most]
        mass, remaining = sum([portions[i] for i in candidates]), surplus
        for i in candidates:
            more = min(most - holding[i], max(1, remaining * portions[i] // mass), surplus)
            holding[i] = holding[i] + more
            surplus = surplus - more
    return np.array(holding)


def scatter_about(own_key, dims, deviation, limit, shards=(), kind=jnp.bfloat16):
    drawn = jax.random.normal(own_key, dims, jnp.float32) * deviation
    if len(shards) > 0:
        drawn = steps_of(own_key, dims, shards, -0.22, 0.18) * drawn
    return jnp.clip(drawn, min=-limit, max=limit).astype(kind)


def setup_inputs(seed: int = 0) -> dict:
    arg_keys = jax.random.split(jax.random.key(seed), 16)
    hidden_in = draw_hidden_in(jax.random.fold_in(arg_keys[15], 71), 0)
    next_embed = draw_next_embed(jax.random.fold_in(arg_keys[15], 71), 0)
    expert_rows = scatter_about(arg_keys[2], (EXPERTS, N_EP, CAP, D), 1.0, 6.0, ((0, 64), (3, 4)))
    routes_keys = jax.random.split(jax.random.fold_in(arg_keys[3], 1), TOKENS // TOK_DEV)
    routes_turns = jax.random.permutation(jax.random.fold_in(arg_keys[3], 3), TOKENS // TOK_DEV)
    routes = jax.vmap(lambda own, number: shared_out(jax.random.fold_in(arg_keys[3], 2), own, number, TOK_DEV, EXPERTS, TOP, CAP, 2))(routes_keys, routes_turns).reshape((TOKENS, TOP))
    gates = jnp.clip(0.05 + 0.45 * jax.random.uniform(arg_keys[4], (TOKENS, TOP), jnp.float32) ** steps_of(arg_keys[4], (TOKENS, TOP), ((0, 64),), -0.2, 0.2), 0.05, 0.5)
    gain_hidden = jnp.clip(0.5 + 1.0 * jax.random.uniform(arg_keys[5], (D,), jnp.float32) ** steps_of(arg_keys[5], (D,), ((0, 4),), -0.2, 0.2), 0.5, 1.5)
    gain_embed = jnp.clip(0.5 + 1.0 * jax.random.uniform(arg_keys[6], (D,), jnp.float32) ** steps_of(arg_keys[6], (D,), ((0, 4),), -0.2, 0.2), 0.5, 1.5)
    join_hidden = draw_join_hidden(jax.random.fold_in(arg_keys[15], 71), 0)
    join_embed = draw_join_embed(jax.random.fold_in(arg_keys[15], 71), 0)
    gain_block = jnp.clip(0.5 + 1.0 * jax.random.uniform(arg_keys[9], (D,), jnp.float32) ** steps_of(arg_keys[9], (D,), ((0, 4),), -0.2, 0.2), 0.5, 1.5)
    down_weight = scatter_about(arg_keys[10], (D, QL + KL + ROPE), D ** -0.5, 0.09375, ((0, 256),))
    gain_query = jnp.clip(jax.random.uniform(arg_keys[11], (QL,), jnp.float32, 0.5, 1.5), 0.5, 1.5)
    gain_latent = jnp.clip(jax.random.uniform(arg_keys[12], (KL,), jnp.float32, 0.5, 1.5), 0.5, 1.5)
    query_up = draw_query_up(jax.random.fold_in(arg_keys[15], 71), 0)
    latent_up = draw_latent_up(jax.random.fold_in(arg_keys[15], 71), 0)
    return dict(hidden_in=hidden_in, next_embed=next_embed, expert_rows=expert_rows, routes=routes, gates=gates, gain_hidden=gain_hidden, gain_embed=gain_embed, join_hidden=join_hidden, join_embed=join_embed, gain_block=gain_block, down_weight=down_weight, gain_query=gain_query, gain_latent=gain_latent, query_up=query_up, latent_up=latent_up)


EPS = 1e-06

def slot_numbers(flat_routes, count):
    experts = jnp.arange(count, dtype=jnp.int32)
    onehot = (flat_routes[:, None] == experts[None, :]).astype(jnp.int32)
    before = jnp.cumsum(onehot, axis=0) - onehot
    return lax.optimization_barrier(jnp.sum(before * onehot, axis=1)).astype(jnp.int32)

def angles(position):
    half = ROPE // 2
    freq = 10000.0 ** (-jnp.arange(half, dtype=jnp.float32) / half)
    phase = position[:, None] * freq[None, :]
    return (jnp.cos(phase), jnp.sin(phase))

def rotate(values, cosine, sine):
    half = values.shape[-1] // 2
    first = values[..., :half]
    second = values[..., half:]
    return jnp.concatenate([first * cosine - second * sine, first * sine + second * cosine], axis=-1)

def rms_norm(values, gain):
    return values * lax.rsqrt(lax.optimization_barrier(jnp.mean(values * values, axis=-1, keepdims=True)) + EPS) * gain

def reference(hidden_in, next_embed, expert_rows, routes, gates, gain_hidden, gain_embed, join_hidden, join_embed, gain_block, down_weight, gain_query, gain_latent, query_up, latent_up):

    def combine_block(block_number):
        block_routes = lax.dynamic_slice_in_dim(routes, block_number * TOK_DEV, TOK_DEV, 0)
        block_gates = lax.dynamic_slice_in_dim(gates, block_number * TOK_DEV, TOK_DEV, 0)
        slots = slot_numbers(block_routes.reshape(-1), EXPERTS).reshape(TOK_DEV, TOP)
        table = expert_rows[:, block_number].reshape(EXPERTS * CAP, D)
        picked = table[(block_routes * CAP + slots).astype(jnp.int32)].astype(jnp.float32)
        return lax.optimization_barrier(jnp.sum(block_gates[:, :, None] * picked, axis=1))
    moe = lax.map(combine_block, jnp.arange(N_EP, dtype=jnp.int32)).reshape(TOKENS, D)
    state = hidden_in.astype(jnp.float32) + moe
    embed = next_embed.astype(jnp.float32)
    norm_hidden = rms_norm(state, gain_hidden).astype(jnp.bfloat16)
    norm_embed = rms_norm(embed, gain_embed).astype(jnp.bfloat16)
    joined = (jnp.dot(norm_hidden, join_hidden, preferred_element_type=jnp.float32) + jnp.dot(norm_embed, join_embed, preferred_element_type=jnp.float32)).astype(jnp.bfloat16)
    normed = rms_norm(joined.astype(jnp.float32), gain_block).astype(jnp.bfloat16)
    down = jnp.dot(normed, down_weight, preferred_element_type=jnp.float32)
    position = (jnp.arange(TOKENS, dtype=jnp.int32) % SEQ_LEN).astype(jnp.float32)
    cosine, sine = angles(position)
    query_latent = rms_norm(down[:, :QL], gain_query).astype(jnp.bfloat16)
    key_latent = rms_norm(down[:, QL:QL + KL], gain_latent).astype(jnp.bfloat16)
    key_rope = rotate(down[:, QL + KL:], cosine, sine).astype(jnp.bfloat16)
    scale = (NOPE + ROPE) ** (-0.5)
    causal = jnp.arange(SEQ_LEN)[None, :] <= jnp.arange(SEQ_LEN)[:, None]

    def one_head(head):
        query_cols = lax.dynamic_slice_in_dim(query_up, head * (NOPE + ROPE), NOPE + ROPE, 1)
        latent_cols = lax.dynamic_slice_in_dim(latent_up, head * (NOPE + VDIM), NOPE + VDIM, 1)
        projected = jnp.dot(query_latent, query_cols, preferred_element_type=jnp.float32)
        q_nope = projected[:, :NOPE].astype(jnp.bfloat16)
        q_rope = rotate(projected[:, NOPE:], cosine, sine).astype(jnp.bfloat16)
        key_values = jnp.dot(key_latent, latent_cols, preferred_element_type=jnp.float32).astype(jnp.bfloat16)
        key_nope = key_values[:, :NOPE]
        values = key_values[:, NOPE:]
        outputs = []
        for sequence in range(SEQS):
            lower = sequence * SEQ_LEN
            upper = lower + SEQ_LEN
            scores = (jnp.dot(q_nope[lower:upper], key_nope[lower:upper].T, preferred_element_type=jnp.float32) + jnp.dot(q_rope[lower:upper], key_rope[lower:upper].T, preferred_element_type=jnp.float32)) * scale
            scores = jnp.where(causal, scores, -jnp.inf)
            highest = lax.optimization_barrier(jnp.max(scores, axis=1, keepdims=True))
            weights = jnp.exp(scores - highest)
            totals = lax.optimization_barrier(jnp.sum(weights, axis=1, keepdims=True))
            outputs.append(jnp.dot(weights.astype(jnp.bfloat16), values[lower:upper], preferred_element_type=jnp.float32) / totals)
        return jnp.concatenate(outputs, axis=0).astype(jnp.bfloat16)
    per_head = lax.map(one_head, jnp.arange(H, dtype=jnp.int32))
    attended = jnp.transpose(per_head, (1, 0, 2)).reshape(TOKENS, H * VDIM)
    return (joined, attended)
```

```python
import functools

import jax
import jax.numpy as jnp
from jax import lax
from jax.experimental import pallas as pl
from jax.experimental.pallas import tpu as pltpu
from jax.sharding import PartitionSpec as P

D = 3584
NOPE = 64
ROPE = 32
VDIM = 64
QL = 768
KL = 256
EPS = 1e-06
NEGATIVE = -1e30
LOG2E = 1.4426950408889634

T = 128
F = 896
HEADS = 16
EP = 64
TP = 4
CAP = 8
EXPERTS = 256
SLOTS = EXPERTS * CAP
PACK = 176
LAT = 384
ROWS = HEADS * T
KB = 512
RC = 512

BF = jnp.bfloat16
F32 = jnp.float32
VMEM = pl.BlockSpec(memory_space=pltpu.VMEM)
ANY = pl.BlockSpec(memory_space=pl.ANY)
MIB = 1 << 20


def params(mib):
    return pltpu.CompilerParams(vmem_limit_bytes=mib * MIB)


def dot(a, b):
    return jnp.dot(a, b, preferred_element_type=F32)


def dot_nt(a, b):
    return lax.dot_general(a, b, (((1,), (1,)), ((), ())), preferred_element_type=F32)


def split3(s):
    hi = s.astype(BF).astype(F32)
    mid = (s - hi).astype(BF).astype(F32)
    low = (s - hi - mid).astype(BF).astype(F32)
    return hi, mid, low


def lanes_of(s, width, first):
    hi, mid, low = split3(s)
    lane = lax.broadcasted_iota(jnp.int32, (s.shape[0], width), 1)
    return jnp.where(
        lane == first,
        hi,
        jnp.where(lane == first + 1, mid, jnp.where(lane == first + 2, low, 0.0)),
    )


def spread_matrix(rows, used, cols):
    row = lax.broadcasted_iota(jnp.int32, (rows, cols), 0)
    col = lax.broadcasted_iota(jnp.int32, (rows, cols), 1)
    part = col & 15
    target = jnp.where(part < used, (col >> 4) * used + part, -1)
    return jnp.where(row == target, 1.0, 0.0).astype(BF)


def features_store(out_ref, state, gain):
    out_ref[:, :F] = (state * gain).astype(BF)
    squares = jnp.sum(state * state, axis=1, keepdims=True)
    out_ref[:, F:] = lanes_of(squares, 128, 0).astype(BF)


def embed_kernel(embed_ref, gain_ref, out_ref):
    features_store(out_ref, embed_ref[...].astype(F32), gain_ref[...])


def combine_kernel(hi_ref, lo_ref, table_ref, hidden_ref, gain_ref, out_ref):
    moe = dot(hi_ref[...], table_ref[...]) + dot(lo_ref[...], table_ref[...])
    features_store(out_ref, hidden_ref[...].astype(F32) + moe, gain_ref[...])


def join_kernel(
    order_ref, h0, h1, h2, h3, e0, e1, e2, e3, gain_ref, packed_ref,
    joined_ref, part_ref, wh, we, wa, wc, sems,
):
    def chunk(half, number, target):
        return pltpu.make_async_copy(
            packed_ref.at[pl.ds(8 * number, 8), half, pl.ds(0, 112), :],
            target.at[pl.ds(8 * number, 8)],
            sems.at[half, number],
        )

    first = [chunk(0, i, wh) for i in range(TP)] + [chunk(1, i, we) for i in range(TP)]
    for copy in first:
        copy.start()
    copy_a = pltpu.make_async_copy(
        packed_ref.at[:, :, pl.ds(112, 16), :], wa, sems.at[2, 0]
    )
    copy_c = pltpu.make_async_copy(
        packed_ref.at[:, :, pl.ds(144, 16), pl.ds(0, 256)], wc, sems.at[2, 1]
    )
    copy_a.start()
    copy_c.start()
    spread = spread_matrix(F, 14, 1024)
    for copy in first:
        copy.wait()

    def project(blocks, weights):
        total = jnp.zeros((T, F), F32)
        squares = jnp.zeros((T, 1), F32)
        for i, block in enumerate(blocks):
            w = weights[pl.ds(8 * order_ref[i], 8)].reshape(F, F)
            total = total + dot(block[:, :F], w)
            squares = squares + jnp.sum(block[:, F:].astype(F32), axis=1, keepdims=True)
        return total * lax.rsqrt(squares / D + EPS)

    joined = (project((h0, h1, h2, h3), wh) + project((e0, e1, e2, e3), we)).astype(BF)
    joined_ref[...] = joined
    wide = joined.astype(F32)
    squares = jnp.sum(wide * wide, axis=1, keepdims=True)
    scaled = dot((wide * gain_ref[...]).astype(BF), spread).astype(BF)
    copy_a.wait()
    copy_c.wait()
    part_ref[:, :F] = dot(scaled, wa[...].reshape(1024, F)).astype(BF)
    rest = dot(scaled, wc[...].reshape(1024, 256))
    part_ref[:, F:] = (rest + lanes_of(squares, 256, 160)).astype(BF)


def rotate_lanes(x, cosine, sine):
    lane = lax.broadcasted_iota(jnp.int32, x.shape, 1)
    width = x.shape[1]
    swapped = jnp.where(
        (lane & 31) < 16, pltpu.roll(x, width - 16, 1), pltpu.roll(x, 16, 1)
    )
    return x * cosine + swapped * sine


def latent_kernel(p0, p1, p2, p3, gq_ref, gl_ref, cos_ref, sin_ref, query_ref, latent_ref):
    total = (p0[...].astype(F32) + p1[...].astype(F32)) + (
        p2[...].astype(F32) + p3[...].astype(F32)
    )
    tail = total[:, 1024:]
    lane = lax.broadcasted_iota(jnp.int32, tail.shape, 1)
    squares = jnp.sum(
        jnp.where((lane >= 32) & (lane < 35), tail, 0.0), axis=1, keepdims=True
    )
    scale = lax.rsqrt(squares / D + EPS)
    query = total[:, :QL] * scale
    query = query * lax.rsqrt(jnp.mean(query * query, axis=1, keepdims=True) + EPS)
    query_ref[...] = (query * gq_ref[...]).astype(BF)
    key = total[:, QL : QL + KL] * scale
    key = key * lax.rsqrt(jnp.mean(key * key, axis=1, keepdims=True) + EPS)
    latent_ref[:, :KL] = (key * gl_ref[...]).astype(BF)
    rope = rotate_lanes(tail * scale, cos_ref[...], sin_ref[...])
    latent_ref[:, KL:] = jnp.where(lane < ROPE, rope, 0.0).astype(BF)


def query_kernel(
    query_ref, cos_ref, sin_ref, packed_ref, out_ref, up_ref, wb, wc, wl, sems
):
    copy_b = pltpu.make_async_copy(packed_ref.at[:, pl.ds(128, 16), :], wb, sems.at[0])
    copy_c = pltpu.make_async_copy(
        packed_ref.at[:, pl.ds(144, 16), pl.ds(256, 640)], wc, sems.at[1]
    )
    copy_l = pltpu.make_async_copy(
        packed_ref.at[:, pl.ds(160, 16), pl.ds(0, 512)], wl, sems.at[2]
    )
    for copy in (copy_b, copy_c, copy_l):
        copy.start()
    spread = spread_matrix(QL, 12, 1024)
    query = dot(query_ref[...], spread).astype(BF)
    row = lax.broadcasted_iota(jnp.int32, (KL, 1024), 0)
    col = lax.broadcasted_iota(jnp.int32, (KL, 1024), 1)
    copy_l.wait()
    gathered = wl[...].reshape(1024, 512)
    for quarter in range(4):
        pick = jnp.where(
            col == (row >> 2) * 16 + quarter * 4 + (row & 3), 1.0, 0.0
        ).astype(BF)
        up_ref[:, pl.ds(512 * quarter, 512)] = dot(pick, gathered).astype(BF)
    copy_b.wait()
    copy_c.wait()
    left = dot(query, wb[...].reshape(1024, F))
    right = dot(query, wc[...].reshape(1024, 640))
    scale = (NOPE + ROPE) ** (-0.5) * LOG2E
    lane = lax.broadcasted_iota(jnp.int32, (T, 128), 1)
    for head in range(HEADS):
        start = NOPE * head
        if start + NOPE <= F:
            nope = left[:, start : start + NOPE]
        else:
            nope = right[:, start - F : start - F + NOPE]
        absorbed = dot_nt(nope.astype(BF), up_ref[:, pl.ds(128 * head, NOPE)])
        out_ref[pl.ds(T * head, T), :KL] = (absorbed * scale).astype(BF)
    for group in range(4):
        x = right[:, 128 + 128 * group : 256 + 128 * group]
        rope = rotate_lanes(x, cos_ref[...], sin_ref[...]) * scale
        for j in range(4):
            own = rope if j == 0 else pltpu.roll(rope, 128 - 32 * j, 1)
            out_ref[pl.ds(T * (4 * group + j), T), KL:] = jnp.where(
                lane < ROPE, own, 0.0
            ).astype(BF)


def attend_kernel(index_ref, q_ref, latent_ref, up_ref, out_ref, m_ref, l_ref, acc_ref):
    block = index_ref[0]
    m_ref[...] = jnp.full(m_ref.shape, NEGATIVE, F32)
    l_ref[...] = jnp.zeros(l_ref.shape, F32)
    acc_ref[...] = jnp.zeros(acc_ref.shape, F32)

    def step(number, masked):
        keys = latent_ref[pl.ds(pl.multiple_of(number * KB, KB), KB), :]
        values = keys[:, :KL]
        for c in range(ROWS // RC):
            rows = pl.ds(c * RC, RC)
            scores = dot_nt(q_ref[rows, :], keys)
            if masked:
                token = lax.broadcasted_iota(jnp.int32, (RC, KB), 0) & (T - 1)
                key = lax.broadcasted_iota(jnp.int32, (RC, KB), 1)
                scores = jnp.where(
                    number * KB + key <= block * T + token, scores, NEGATIVE
                )
            before = m_ref[rows, :]
            highest = jnp.maximum(before, jnp.max(scores, axis=1, keepdims=True))
            factor = jnp.exp2(before - highest)
            weights = jnp.exp2(scores - highest[:, :1])
            l_ref[rows, :] = l_ref[rows, :] * factor + jnp.sum(
                weights, axis=1, keepdims=True
            )
            acc_ref[rows, :] = acc_ref[rows, :] * factor[:, :1] + dot(
                weights.astype(BF), values
            )
            m_ref[rows, :] = highest

    last = (block * T) // KB
    lax.fori_loop(0, last, lambda i, _: step(i, False), None)
    step(last, True)
    for pair in range(HEADS // 2):
        sides = []
        for head in (2 * pair, 2 * pair + 1):
            rows = pl.ds(T * head, T)
            mean = (acc_ref[rows, :] / l_ref[rows, :1]).astype(BF)
            sides.append(dot(mean, up_ref[:, pl.ds(128 * head + NOPE, VDIM)]))
        out_ref[:, pl.ds(128 * pair, 128)] = jnp.concatenate(sides, axis=1).astype(BF)


def ring(x, shift):
    return lax.ppermute(x, "tp", [(i, (i + shift) % TP) for i in range(TP)])


def from_all(x):
    return [x] + [ring(x, shift) for shift in (1, 2, 3)]


def slot_weights(routes, gates):
    experts = jnp.arange(EXPERTS, dtype=jnp.int32)
    onehot = (routes[:, :, None] == experts[None, None, :]).astype(F32)
    named = jnp.sum(onehot, axis=1)
    earlier = jnp.tril(jnp.ones((T, T), BF), -1)
    before = dot(earlier, named.astype(BF))
    slots = jnp.sum(before[:, None, :] * onehot, axis=2).astype(jnp.int32)
    place = routes * CAP + slots
    lane = jnp.arange(SLOTS, dtype=jnp.int32)
    weights = jnp.zeros((T, SLOTS), F32)
    for k in range(routes.shape[1]):
        weights = weights + jnp.where(place[:, k : k + 1] == lane[None], gates[:, k : k + 1], 0.0)
    return weights


def pack_weights(first, down_weight, query_up, latent_up):
    per_head = query_up.reshape(12, HEADS, NOPE + ROPE)
    query = jnp.concatenate(
        [
            per_head[:, :, :NOPE].reshape(12, HEADS * NOPE),
            per_head[:, :, NOPE:].reshape(12, HEADS * ROPE),
        ],
        axis=1,
    )
    group_a = jnp.pad(down_weight[:, :F], ((0, 2), (0, 0)))
    group_b = jnp.pad(query[:, :F], ((0, 4), (0, 0)))
    group_c = jnp.concatenate(
        [
            jnp.pad(down_weight[:, F:], ((0, 2), (0, 96))),
            jnp.pad(query[:, F:], ((0, 4), (0, 0))),
        ],
        axis=1,
    )
    stacked = jnp.concatenate([latent_up[:, 512 * q : 512 * q + 512] for q in range(4)], axis=0)
    group_d = jnp.pad(stacked, ((0, 0), (0, F - 512)))
    return jnp.concatenate([first, group_a, group_b, group_c, group_d], axis=0)


def split_gates_kernel(weights_ref, hi_ref, lo_ref):
    weights = weights_ref[...]
    hi = weights.astype(BF)
    hi_ref[...] = hi
    lo_ref[...] = (weights - hi.astype(F32)).astype(BF)


def shards(
    hidden_in, next_embed, expert_rows, routes, gates, gain_hidden, gain_embed, join_hidden,
    join_embed, gain_block, down_weight, gain_query, gain_latent, query_up, latent_up,
):
    ep = lax.axis_index("ep")
    tp = lax.axis_index("tp")
    even = ep % 2 == 0

    swapped = lax.ppermute(
        jnp.where(even, join_embed, join_hidden), "ep", [(i, i ^ 1) for i in range(EP)]
    )
    first = jnp.concatenate(
        [jnp.where(even, join_hidden, swapped), jnp.where(even, swapped, join_embed)], axis=0
    )
    packed = lax.all_gather(
        pack_weights(first, down_weight, query_up, latent_up), "ep", axis=0, tiled=False
    )

    received = lax.all_to_all(expert_rows, "ep", split_axis=1, concat_axis=0, tiled=True)
    table = received.reshape(SLOTS, F)

    embeds = from_all(
        pl.pallas_call(
            embed_kernel,
            out_shape=jax.ShapeDtypeStruct((T, 1024), BF),
            in_specs=[VMEM] * 2,
            out_specs=VMEM,
            name="embed",
        )(next_embed, gain_embed[None])
    )
    hi, lo = pl.pallas_call(
        split_gates_kernel,
        out_shape=[jax.ShapeDtypeStruct((T, SLOTS), BF)] * 2,
        in_specs=[VMEM],
        out_specs=[VMEM] * 2,
        name="split_gates",
    )(slot_weights(routes, gates))

    position = (ep * T + jnp.arange(T, dtype=jnp.int32)).astype(F32)
    freq = 10000.0 ** (-jnp.arange(ROPE // 2, dtype=F32) / (ROPE // 2))
    phase = position[:, None] * freq[None, :]
    cosine = jnp.tile(jnp.cos(phase), (1, 8))
    sine = jnp.tile(jnp.concatenate([-jnp.sin(phase), jnp.sin(phase)], axis=1), (1, 4))

    hiddens = from_all(
        pl.pallas_call(
            combine_kernel,
            out_shape=jax.ShapeDtypeStruct((T, 1024), BF),
            in_specs=[VMEM] * 5,
            out_specs=VMEM,
            compiler_params=params(32),
            name="combine",
        )(hi, lo, table, hidden_in, gain_hidden[None])
    )
    order = jnp.mod(tp - jnp.arange(TP, dtype=jnp.int32), TP)
    joined, part = pl.pallas_call(
        join_kernel,
        out_shape=[
            jax.ShapeDtypeStruct((T, F), BF),
            jax.ShapeDtypeStruct((T, 1152), BF),
        ],
        in_specs=[pl.BlockSpec(memory_space=pltpu.SMEM)] + [VMEM] * 9 + [ANY],
        out_specs=[VMEM] * 2,
        scratch_shapes=[
            pltpu.VMEM((EP // 2, 112, F), BF),
            pltpu.VMEM((EP // 2, 112, F), BF),
            pltpu.VMEM((EP // 2, 2, 16, F), BF),
            pltpu.VMEM((EP // 2, 2, 16, 256), BF),
            pltpu.SemaphoreType.DMA((3, 4)),
        ],
        compiler_params=params(48),
        name="join",
    )(order, *hiddens, *embeds, gain_block[None], packed.reshape(EP // 2, 2, PACK, F))

    query_latent, latent = pl.pallas_call(
        latent_kernel,
        out_shape=[
            jax.ShapeDtypeStruct((T, QL), BF),
            jax.ShapeDtypeStruct((T, LAT), BF),
        ],
        in_specs=[VMEM] * 8,
        out_specs=[VMEM] * 2,
        name="latent",
    )(*from_all(part), gain_query[None], gain_latent[None], cosine, sine)
    latents = lax.all_gather(latent, "ep", axis=0, tiled=True)
    queries, up = pl.pallas_call(
        query_kernel,
        out_shape=[
            jax.ShapeDtypeStruct((ROWS, LAT), BF),
            jax.ShapeDtypeStruct((KL, HEADS * 128), BF),
        ],
        in_specs=[VMEM] * 3 + [ANY],
        out_specs=[VMEM] * 2,
        scratch_shapes=[
            pltpu.VMEM((EP, 16, F), BF),
            pltpu.VMEM((EP, 16, 640), BF),
            pltpu.VMEM((EP, 16, 512), BF),
            pltpu.SemaphoreType.DMA((3,)),
        ],
        compiler_params=params(48),
        name="query",
    )(query_latent, cosine, sine, packed)
    attended = pl.pallas_call(
        attend_kernel,
        out_shape=jax.ShapeDtypeStruct((T, HEADS * VDIM), BF),
        in_specs=[pl.BlockSpec(memory_space=pltpu.SMEM)] + [VMEM] * 3,
        out_specs=VMEM,
        scratch_shapes=[
            pltpu.VMEM((ROWS, 128), F32),
            pltpu.VMEM((ROWS, 128), F32),
            pltpu.VMEM((ROWS, KL), F32),
        ],
        compiler_params=params(56),
        name="attend",
    )(ep[None], queries, latents, up)
    return (joined, attended)


def solution(mesh):
    placed = (
        P("ep", "tp"),
        P("ep", "tp"),
        P("ep", None, None, "tp"),
        P("ep", None),
        P("ep", None),
        P("tp"),
        P("tp"),
        P("ep", "tp"),
        P("ep", "tp"),
        P("tp"),
        P(("tp", "ep"), None),
        P(),
        P(),
        P("ep", "tp"),
        P("ep", "tp"),
    )
    return jax.shard_map(
        shards,
        mesh=mesh,
        in_specs=placed,
        out_specs=(P("ep", "tp"), P("ep", "tp")),
        check_vma=False,
    )
```

```python
import functools

import jax
import jax.numpy as jnp
from jax import lax
from jax.experimental import pallas as pl
from jax.experimental.pallas import tpu as pltpu
from jax.sharding import PartitionSpec as P

D = 3584
NOPE = 64
ROPE = 32
VDIM = 64
QL = 768
KL = 256
EPS = 1e-06
NEGATIVE = -1e30
LOG2E = 1.4426950408889634

T = 128
F = 896
HEADS = 16
EP = 64
TP = 4
CAP = 8
EXPERTS = 256
SLOTS = EXPERTS * CAP
PACK = 160
LAT = KL + ROPE
ROWS = HEADS * T
ZS, YS = 8, 4
KEYS = ZS * T
COLS = 1024

BF = jnp.bfloat16
F32 = jnp.float32
VMEM = pl.BlockSpec(memory_space=pltpu.VMEM)
HBM = pl.BlockSpec(memory_space=pltpu.HBM)
MIB = 1 << 20


def params(mib):
    return pltpu.CompilerParams(vmem_limit_bytes=mib * MIB)


def dot(a, b):
    return jnp.dot(a, b, preferred_element_type=F32)


def dot_nt(a, b):
    return lax.dot_general(a, b, (((1,), (1,)), ((), ())), preferred_element_type=F32)


def split3(s):
    hi = s.astype(BF).astype(F32)
    mid = (s - hi).astype(BF).astype(F32)
    low = (s - hi - mid).astype(BF).astype(F32)
    return hi, mid, low


def lanes_of(s, width, first):
    hi, mid, low = split3(s)
    lane = lax.broadcasted_iota(jnp.int32, (s.shape[0], width), 1)
    return jnp.where(
        lane == first,
        hi,
        jnp.where(lane == first + 1, mid, jnp.where(lane == first + 2, low, 0.0)),
    )


def spread_matrix(rows, used, width, cols, skip=0):
    row = lax.broadcasted_iota(jnp.int32, (rows, cols), 0)
    col = lax.broadcasted_iota(jnp.int32, (rows, cols), 1)
    part = (col & (width - 1)) - skip
    target = jnp.where(
        (part >= 0) & (part < used), (col >> (width.bit_length() - 1)) * used + part, -1
    )
    return jnp.where(row == target, 1.0, 0.0).astype(BF)


def features_store(out_ref, state, gain, skip):
    spread = spread_matrix(F, 56, 64, 1024, skip)
    squares = jnp.sum(state * state, axis=1, keepdims=True)
    scaled = dot((state * gain).astype(BF), spread)
    lanes = lanes_of(squares, 128, 0 if skip else 56)
    out_ref[:, :128] = (scaled[:, :128] + lanes).astype(BF)
    out_ref[:, 128:] = scaled[:, 128:].astype(BF)


def embed_kernel(embed_ref, gain_ref, out_ref):
    features_store(out_ref, embed_ref[...].astype(F32), gain_ref[...], 8)


def combine_kernel(hi_ref, lo_ref, table_ref, hidden_ref, gain_ref, out_ref):
    moe = dot(hi_ref[...], table_ref[...]) + dot(lo_ref[...], table_ref[...])
    features_store(out_ref, hidden_ref[...].astype(F32) + moe, gain_ref[...], 0)


def join_kernel(
    order_ref, h0, h1, h2, h3, e0, e1, e2, e3, gain_ref, packed_ref,
    joined_ref, latent_ref, query_ref, wh, we, wa, wc, sems,
):
    def chunk(half, first, number, target):
        rows = pl.ds(pl.multiple_of(16 * order_ref[number], 16), 16)
        return pltpu.make_async_copy(
            packed_ref.at[rows, pl.ds(first, 64), :],
            target.at[pl.ds(16 * number, 16)],
            sems.at[half, number],
        )

    copies_e = [chunk(1, 48, i, we) for i in range(TP)]
    copies_h = [chunk(0, 0, i, wh) for i in range(TP)]
    copy_a = pltpu.make_async_copy(packed_ref.at[:, pl.ds(112, 16), :], wa, sems.at[2, 0])
    copy_c = pltpu.make_async_copy(
        packed_ref.at[:, pl.ds(144, 16), pl.ds(0, 256)], wc, sems.at[2, 1]
    )
    for copy in copies_e + copies_h + [copy_a, copy_c]:
        copy.start()
    spread = spread_matrix(F, 14, 16, 1024)
    lane = lax.broadcasted_iota(jnp.int32, (T, 1024), 1) & 63

    def project(blocks, weights, copies, used):
        total = jnp.zeros((T, F), F32)
        squares = jnp.zeros((T, 1), F32)
        for i, ref in enumerate(blocks):
            block = ref[...].astype(F32)
            held = jnp.where(used[:, :128], 0.0, block[:, :128])
            squares = squares + jnp.sum(held, axis=1, keepdims=True)
            block = jnp.where(used, block, 0.0).astype(BF)
            copies[i].wait()
            weight = weights[pl.ds(16 * i, 16)].reshape(1024, F)
            total = total + dot(block, weight)
        return total * lax.rsqrt(squares / D + EPS)

    embed = project((e0, e1, e2, e3), we, copies_e, lane >= 8)
    joined = (project((h0, h1, h2, h3), wh, copies_h, lane < 56) + embed).astype(BF)
    joined_ref[...] = joined
    wide = joined.astype(F32)
    squares = jnp.sum(wide * wide, axis=1, keepdims=True)
    scaled = dot((wide * gain_ref[...]).astype(BF), spread).astype(BF)
    copy_a.wait()
    copy_c.wait()
    down = dot(scaled, wa[...].reshape(1024, F))
    query_ref[...] = down[:, :QL].astype(BF)
    latent_ref[:, :128] = down[:, QL:].astype(BF)
    tail = dot(scaled, wc[...].reshape(1024, 256))
    latent_ref[:, 128:] = (tail + lanes_of(squares, 256, 160)).astype(BF)


def rotate(x, cos_ref, sin_ref):
    first, second = x[: ROPE // 2], x[ROPE // 2 :]
    cosine, sine = cos_ref[...], sin_ref[...]
    return jnp.concatenate(
        [first * cosine - second * sine, first * sine + second * cosine], axis=0
    )


def add_parts(refs):
    a, b, c, d = (ref[...].astype(F32) for ref in refs)
    return (a + b) + (c + d)


def latent_kernel(p0, p1, p2, p3, gl_ref, cos_ref, sin_ref, latent_ref, scale_ref):
    total = add_parts((p0, p1, p2, p3))
    tail = total[:, KL:]
    lane = lax.broadcasted_iota(jnp.int32, tail.shape, 1)
    squares = jnp.sum(
        jnp.where((lane >= 32) & (lane < 35), tail, 0.0), axis=1, keepdims=True
    )
    scale = lax.rsqrt(squares / D + EPS)
    key = total[:, :KL] * scale
    key = key * lax.rsqrt(jnp.mean(key * key, axis=1, keepdims=True) + EPS)
    latent_ref[:KL, :] = jnp.transpose(key * gl_ref[...]).astype(BF)
    rope = rotate(jnp.transpose(tail * scale)[:ROPE], cos_ref, sin_ref)
    latent_ref[KL:, :] = rope.astype(BF)
    scale_ref[...] = jnp.broadcast_to(scale, (T, 128))


def up_kernel(packed_ref, key_ref, value_ref, held, sem):
    copy = pltpu.make_async_copy(packed_ref.at[:, pl.ds(112, 48), :], held, sem)
    copy.start()
    row = lax.broadcasted_iota(jnp.int32, (KL, 1024), 0)
    col = lax.broadcasted_iota(jnp.int32, (KL, 1024), 1) - (row >> 2) * 16
    row = row & 3

    def pick(target):
        return jnp.where(col == target, 1.0, 0.0).astype(BF)

    copy.wait()
    group_a = held[:, 0:16, 0:768].reshape(1024, 768)
    group_b = held[:, 16:32, :].reshape(1024, F)
    group_c = held[:, 32:48, 256:].reshape(1024, 640)
    group_d = held[:, 32:48, :256].reshape(1024, 256)
    spare = pick(12 + row)
    even = pick(jnp.where(row & 1 == 0, 14 + (row >> 1), -9999))
    odd = pick(jnp.where(row & 1 == 1, 14 + (row >> 1), -9999))
    up = jnp.concatenate(
        [
            dot(spare, group_b),
            dot(spare, group_c),
            dot(even, group_a[:, :384]) + dot(odd, group_a[:, 384:]),
            dot(even, group_d[:, :128]) + dot(odd, group_d[:, 128:]),
        ],
        axis=1,
    )
    for head in range(HEADS):
        own = up[:, 128 * head : 128 * head + 128]
        key_ref[:, pl.ds(128 * head, 128)] = own.astype(BF)
        value_ref[pl.ds(VDIM * head, VDIM), :] = jnp.transpose(own)[NOPE:, :].astype(BF)


def query_kernel(
    q0, q1, q2, q3, scale_ref, gq_ref, cos_ref, sin_ref, up_ref, packed_ref, out_ref, held, sem
):
    copy = pltpu.make_async_copy(packed_ref.at[:, pl.ds(128, 32), :], held, sem)
    copy.start()
    spread = spread_matrix(QL, 12, 16, 1024)
    query = add_parts((q0, q1, q2, q3)) * scale_ref[:, :1]
    query = query * lax.rsqrt(jnp.mean(query * query, axis=1, keepdims=True) + EPS)
    query = dot((query * gq_ref[...]).astype(BF), spread).astype(BF)
    copy.wait()
    group_b = held[:, 0:16, :].reshape(1024, F)
    group_c = held[:, 16:32, 256:].reshape(1024, 640)
    projected = jnp.transpose(
        jnp.concatenate([dot(query, group_b), dot(query, group_c)], axis=1)
    )
    scale = (NOPE + ROPE) ** (-0.5) * LOG2E
    width = NOPE + ROPE
    for head in range(HEADS):
        nope = projected[width * head : width * head + NOPE].astype(BF)
        absorbed = dot(up_ref[:, pl.ds(128 * head, NOPE)], nope)
        cols = pl.ds(T * head, T)
        out_ref[:KL, cols] = (absorbed * scale).astype(BF)
        rope = rotate(projected[width * head + NOPE : width * head + width], cos_ref, sin_ref)
        out_ref[KL:, cols] = (rope * scale).astype(BF)


def attend_kernel(chunks, first, last, index_ref, q_ref, *rest):
    count = len(chunks)
    latents, rest = rest[:count], rest[count:]
    if last:
        up_ref, rest = rest[0], rest[1:]
    if not first:
        (m_in, l_in, acc_in), rest = rest[:3], rest[3:]
    if last:
        out_ref, rest = rest[0], rest[1:]
        m_ref, l_ref, acc_ref, keys, values = rest
    else:
        m_ref, l_ref, acc_ref, keys, values = rest
    ep = index_ref[0]
    z, y, core = ep >> 3, (ep >> 1) & 3, ep & 1

    for number, (dy, dc) in enumerate(chunks):
        fresh = first and number == 0
        diagonal = dy == 0 and dc == 0
        for i in range(ZS):
            block = latents[number][i]
            keys[pl.ds(T * i, T), :] = jnp.transpose(block)
            values[:, pl.ds(T * i, T)] = block[:KL, :]
        before = ((y - dy) & 3) * 2 + (core ^ dc) <= y * 2 + core
        hidden = [
            jnp.where(dz <= z if dz else before, 0.0, NEGATIVE) for dz in ALONG_Z
        ]

        def step(i):
            cols = pl.ds(i * COLS, COLS)
            scores = dot(keys[...], q_ref[:, cols])
            blocks = [scores[T * i : T * i + T] for i in range(ZS)]
            if diagonal:
                key = lax.broadcasted_iota(jnp.int32, (T, COLS), 0)
                token = lax.broadcasted_iota(jnp.int32, (T, COLS), 1) & (T - 1)
                own = ALONG_Z.index(0)
                blocks[own] = jnp.where(key <= token, blocks[own], NEGATIVE)
            highest = [
                jnp.max(block, axis=0, keepdims=True) + bias
                for block, bias in zip(blocks, hidden)
            ]
            highest = functools.reduce(jnp.maximum, highest)
            if not fresh:
                if first or number > 0:
                    m_old, l_old, acc_old = m_ref[:, cols], l_ref[:, cols], acc_ref[:, cols]
                else:
                    m_old, l_old, acc_old = m_in[:, cols], l_in[:, cols], acc_in[:, cols]
                highest = jnp.maximum(highest, m_old)
                factor = jnp.exp2(m_old - highest)
            weights = [
                jnp.exp2(block - (highest - bias)) for block, bias in zip(blocks, hidden)
            ]
            total = functools.reduce(
                jnp.add, [jnp.sum(w, axis=0, keepdims=True) for w in weights]
            )
            added = dot(
                values[...], jnp.concatenate([w.astype(BF) for w in weights], axis=0)
            )
            if not fresh:
                total = total + l_old * factor
                added = added + acc_old * factor
            m_ref[:, cols] = highest
            l_ref[:, cols] = total
            acc_ref[:, cols] = added

        for i in range(ROWS // COLS):
            step(i)
    if last:
        outs = []
        for head in range(HEADS):
            cols = pl.ds(T * head, T)
            mean = (acc_ref[:, cols] / l_ref[:, cols]).astype(BF)
            outs.append(dot(up_ref[pl.ds(VDIM * head, VDIM), :], mean))
        out_ref[...] = jnp.transpose(jnp.concatenate(outs, axis=0)).astype(BF)


def attend(ep, queries, up, chunks, first, last, latents, state):
    carried = [
        jax.ShapeDtypeStruct((1, ROWS), F32),
        jax.ShapeDtypeStruct((1, ROWS), F32),
        jax.ShapeDtypeStruct((KL, ROWS), F32),
    ]
    args = [ep[None], queries, *latents]
    if last:
        args.append(up)
    aliases = {}
    if not first:
        if not last:
            aliases = {len(args) + i: i for i in range(3)}
        args += state
    scratch = [pltpu.VMEM((KEYS, LAT), BF), pltpu.VMEM((KL, KEYS), BF)]
    if last:
        out_shape = [jax.ShapeDtypeStruct((T, HEADS * VDIM), BF)]
        scratch = [pltpu.VMEM(s.shape, F32) for s in carried] + scratch
    else:
        out_shape = carried
    return pl.pallas_call(
        functools.partial(attend_kernel, chunks, first, last),
        out_shape=out_shape,
        in_specs=[pl.BlockSpec(memory_space=pltpu.SMEM)] + [VMEM] * (len(args) - 1),
        out_specs=[VMEM] * len(out_shape),
        scratch_shapes=scratch,
        input_output_aliases=aliases,
        compiler_params=params(32),
        name="attend",
    )(*args)


def ring(x, shift):
    return lax.ppermute(x, "tp", [(i, (i + shift) % TP) for i in range(TP)])


def from_all(x):
    return [x] + [ring(x, shift) for shift in (1, 2, 3)]


def along_z(x, shift):
    return lax.ppermute(x, "ep", [(i, (i + 8 * shift) % EP) for i in range(EP)])


def along_y(x, shift):
    pairs = [(i, (i & ~6) | ((i + 2 * shift) & 6)) for i in range(EP)]
    return lax.ppermute(x, "ep", pairs)


def other_core(x):
    return lax.ppermute(x, "ep", [(i, i ^ 1) for i in range(EP)])


ALONG_Z = (1, 0, 7, 4, 3, 2, 6, 5)


def z_blocks(x):
    three = jnp.stack([along_z(x, 1), x, along_z(x, -1)])
    return jnp.concatenate([three, along_z(three, 3), along_z(three[:2], -3)], axis=0)


def slot_weights(routes, gates):
    experts = jnp.arange(EXPERTS, dtype=jnp.int32)
    onehot = (routes[:, :, None] == experts[None, None, :]).astype(F32)
    named = jnp.sum(onehot, axis=1)
    earlier = jnp.tril(jnp.ones((T, T), BF), -1)
    before = dot(earlier, named.astype(BF))
    slots = jnp.sum(before[:, None, :] * onehot, axis=2).astype(jnp.int32)
    place = routes * CAP + slots
    lane = jnp.arange(SLOTS, dtype=jnp.int32)
    weights = jnp.zeros((T, SLOTS), F32)
    for k in range(routes.shape[1]):
        weights = weights + jnp.where(place[:, k : k + 1] == lane[None], gates[:, k : k + 1], 0.0)
    return weights


def pack_kernel(hidden_ref, embed_ref, down_ref, query_ref, latent_ref, out_ref):
    hidden, embed, down, query, latent = (
        ref[...].astype(F32) for ref in (hidden_ref, embed_ref, down_ref, query_ref, latent_ref)
    )
    rows = [latent[r : r + 1] for r in range(4)]
    out_ref[pl.ds(0, 112), :] = jnp.concatenate([hidden, embed], axis=0).astype(BF)
    spare = jnp.zeros((1, 128), F32)
    group_1 = jnp.concatenate(
        [
            down[:, :F],
            jnp.concatenate([rows[0][:, 1536:1920], rows[1][:, 1536:1920], spare], axis=1),
            jnp.concatenate([rows[2][:, 1536:1920], rows[3][:, 1536:1920], spare], axis=1),
        ],
        axis=0,
    )
    out_ref[pl.ds(112, 16), :] = group_1.astype(BF)
    group_2 = jnp.concatenate([query[:, :F], latent[:, :F]], axis=0)
    out_ref[pl.ds(128, 16), :] = group_2.astype(BF)
    tail = jnp.concatenate([down[:, F:], jnp.zeros((14, 96), F32)], axis=1)
    left = jnp.concatenate(
        [
            tail,
            jnp.concatenate([rows[0][:, 1920:], rows[1][:, 1920:]], axis=1),
            jnp.concatenate([rows[2][:, 1920:], rows[3][:, 1920:]], axis=1),
        ],
        axis=0,
    )
    right = jnp.concatenate([query[:, F:], latent[:, F:1536]], axis=0)
    out_ref[pl.ds(144, 16), :] = jnp.concatenate([left, right], axis=1).astype(BF)


def split_gates_kernel(weights_ref, hi_ref, lo_ref):
    weights = weights_ref[...]
    hi = weights.astype(BF)
    hi_ref[...] = hi
    lo_ref[...] = (weights - hi.astype(F32)).astype(BF)


def shards(
    hidden_in, next_embed, expert_rows, routes, gates, gain_hidden, gain_embed, join_hidden,
    join_embed, gain_block, down_weight, gain_query, gain_latent, query_up, latent_up,
):
    ep = lax.axis_index("ep")
    tp = lax.axis_index("tp")
    order = jnp.mod(tp - jnp.arange(TP, dtype=jnp.int32), TP)
    order = jnp.concatenate([order, ep[None]])
    smem = pl.BlockSpec(memory_space=pltpu.SMEM)

    packed = lax.all_gather(
        pl.pallas_call(
            pack_kernel,
            out_shape=jax.ShapeDtypeStruct((PACK, F), BF),
            in_specs=[VMEM] * 5,
            out_specs=VMEM,
            name="pack",
        )(join_hidden, join_embed, down_weight, query_up, latent_up),
        "ep",
        axis=0,
        tiled=False,
    )
    received = lax.all_to_all(expert_rows, "ep", split_axis=1, concat_axis=0, tiled=True)
    table = received.reshape(SLOTS, F)

    embeds = from_all(
        pl.pallas_call(
            embed_kernel,
            out_shape=jax.ShapeDtypeStruct((T, 1024), BF),
            in_specs=[VMEM] * 2,
            out_specs=VMEM,
            name="embed",
        )(next_embed, gain_embed[None])
    )
    hi, lo = pl.pallas_call(
        split_gates_kernel,
        out_shape=[jax.ShapeDtypeStruct((T, SLOTS), BF)] * 2,
        in_specs=[VMEM],
        out_specs=[VMEM] * 2,
        name="split_gates",
    )(slot_weights(routes, gates))

    position = (ep * T + jnp.arange(T, dtype=jnp.int32)).astype(F32)
    freq = 10000.0 ** (-jnp.arange(ROPE // 2, dtype=F32) / (ROPE // 2))
    phase = freq[:, None] * position[None, :]
    cosine = jnp.cos(phase)
    sine = jnp.sin(phase)

    hiddens = from_all(
        pl.pallas_call(
            combine_kernel,
            out_shape=jax.ShapeDtypeStruct((T, 1024), BF),
            in_specs=[VMEM] * 5,
            out_specs=VMEM,
            compiler_params=params(32),
            name="combine",
        )(hi, lo, table, hidden_in, gain_hidden[None])
    )
    joined, part, query_part = pl.pallas_call(
        join_kernel,
        out_shape=[
            jax.ShapeDtypeStruct((T, F), BF),
            jax.ShapeDtypeStruct((T, KL + 128), BF),
            jax.ShapeDtypeStruct((T, QL), BF),
        ],
        in_specs=[smem] + [VMEM] * 9 + [HBM],
        out_specs=[VMEM] * 3,
        scratch_shapes=[
            pltpu.VMEM((EP, 64, F), BF),
            pltpu.VMEM((EP, 64, F), BF),
            pltpu.VMEM((EP, 16, F), BF),
            pltpu.VMEM((EP, 16, 256), BF),
            pltpu.SemaphoreType.DMA((3, 4)),
        ],
        compiler_params=params(50),
        name="join",
    )(order, *hiddens, *embeds, gain_block[None], packed)

    later, part = lax.optimization_barrier((packed, part))
    key_up, value_up = pl.pallas_call(
        up_kernel,
        out_shape=[
            jax.ShapeDtypeStruct((KL, HEADS * 128), BF),
            jax.ShapeDtypeStruct((HEADS * VDIM, KL), BF),
        ],
        in_specs=[HBM],
        out_specs=[VMEM] * 2,
        scratch_shapes=[pltpu.VMEM((EP, 48, F), BF), pltpu.SemaphoreType.DMA],
        compiler_params=params(50),
        name="up",
    )(later)
    latent, scale = pl.pallas_call(
        latent_kernel,
        out_shape=[jax.ShapeDtypeStruct((LAT, T), BF), jax.ShapeDtypeStruct((T, 128), F32)],
        in_specs=[VMEM] * 7,
        out_specs=[VMEM] * 2,
        name="latent",
    )(*from_all(part), gain_latent[None], cosine, sine)
    queries = pl.pallas_call(
        query_kernel,
        out_shape=jax.ShapeDtypeStruct((LAT, ROWS), BF),
        in_specs=[VMEM] * 9 + [HBM],
        out_specs=VMEM,
        scratch_shapes=[pltpu.VMEM((EP, 32, F), BF), pltpu.SemaphoreType.DMA],
        compiler_params=params(50),
        name="query",
    )(*from_all(query_part), scale, gain_query[None], cosine, sine, key_up, packed)
    column, queries = lax.optimization_barrier((z_blocks(latent), queries))
    chunk_1, chunk_3 = along_y(column, 1), along_y(column, -1)
    call = functools.partial(attend, ep, queries, value_up)
    state = call(((0, 0), (0, 1)), True, False, (column, other_core(column)), None)
    chunk_1, chunk_3, state = lax.optimization_barrier((chunk_1, chunk_3, state))
    halves = along_y(chunk_1[:4], 1), along_y(chunk_3[4:], -1)
    far_1, far_3 = other_core(chunk_1), other_core(chunk_3)
    state = call(((1, 0), (3, 0)), False, False, (chunk_1, chunk_3), state)
    halves, state = lax.optimization_barrier((halves, state))
    chunk_2 = jnp.concatenate(halves)
    far_2 = other_core(chunk_2)
    state = call(((1, 1), (3, 1)), False, False, (far_1, far_3), state)
    (attended,) = call(((2, 0), (2, 1)), False, True, (chunk_2, far_2), state)
    return (joined, attended)


def solution(mesh):
    placed = (
        P("ep", "tp"),
        P("ep", "tp"),
        P("ep", None, None, "tp"),
        P("ep", None),
        P("ep", None),
        P("tp"),
        P("tp"),
        P("ep", "tp"),
        P("ep", "tp"),
        P("tp"),
        P(("tp", "ep"), None),
        P(),
        P(),
        P("ep", "tp"),
        P("ep", "tp"),
    )
    return jax.shard_map(
        shards,
        mesh=mesh,
        in_specs=placed,
        out_specs=(P("ep", "tp"), P("ep", "tp")),
        check_vma=False,
    )
```

```python
import functools

import jax
import jax.numpy as jnp
from jax import lax
from jax.experimental import pallas as pl
from jax.experimental.pallas import tpu as pltpu
from jax.sharding import PartitionSpec as P

D = 3584
NOPE = 64
ROPE = 32
VDIM = 64
QL = 768
KL = 256
EPS = 1e-06
NEGATIVE = -1e30
LOG2E = 1.4426950408889634

T = 128
F = 896
HEADS = 16
EP = 64
TP = 4
CAP = 8
EXPERTS = 256
SLOTS = EXPERTS * CAP
PACK = 160
LAT = KL + ROPE
ROWS = HEADS * T
ZS, YS = 8, 4
KEYS = ZS * T
COLS = 1024

BF = jnp.bfloat16
F32 = jnp.float32
VMEM = pl.BlockSpec(memory_space=pltpu.VMEM)
HBM = pl.BlockSpec(memory_space=pltpu.HBM)
MIB = 1 << 20


def params(mib):
    return pltpu.CompilerParams(vmem_limit_bytes=mib * MIB)


def dot(a, b):
    return jnp.dot(a, b, preferred_element_type=F32)


def dot_nt(a, b):
    return lax.dot_general(a, b, (((1,), (1,)), ((), ())), preferred_element_type=F32)


def split3(s):
    hi = s.astype(BF).astype(F32)
    mid = (s - hi).astype(BF).astype(F32)
    low = (s - hi - mid).astype(BF).astype(F32)
    return hi, mid, low


def lanes_of(s, width, first):
    hi, mid, low = split3(s)
    lane = lax.broadcasted_iota(jnp.int32, (s.shape[0], width), 1)
    return jnp.where(
        lane == first,
        hi,
        jnp.where(lane == first + 1, mid, jnp.where(lane == first + 2, low, 0.0)),
    )


def spread_matrix(rows, used, width, cols, skip=0):
    row = lax.broadcasted_iota(jnp.int32, (rows, cols), 0)
    col = lax.broadcasted_iota(jnp.int32, (rows, cols), 1)
    part = (col & (width - 1)) - skip
    target = jnp.where(
        (part >= 0) & (part < used), (col >> (width.bit_length() - 1)) * used + part, -1
    )
    return jnp.where(row == target, 1.0, 0.0).astype(BF)


def features_store(out_ref, state, gain, skip):
    spread = spread_matrix(F, 56, 64, 1024, skip)
    squares = jnp.sum(state * state, axis=1, keepdims=True)
    scaled = dot((state * gain).astype(BF), spread)
    lanes = lanes_of(squares, 128, 0 if skip else 56)
    out_ref[:, :128] = (scaled[:, :128] + lanes).astype(BF)
    out_ref[:, 128:] = scaled[:, 128:].astype(BF)


def embed_kernel(embed_ref, gain_ref, out_ref):
    features_store(out_ref, embed_ref[...].astype(F32), gain_ref[...], 8)


def combine_kernel(hi_ref, lo_ref, table_ref, hidden_ref, gain_ref, out_ref):
    moe = dot(hi_ref[...], table_ref[...]) + dot(lo_ref[...], table_ref[...])
    features_store(out_ref, hidden_ref[...].astype(F32) + moe, gain_ref[...], 0)


def join_kernel(
    order_ref, h0, h1, h2, h3, e0, e1, e2, e3, gain_ref, packed_ref,
    joined_ref, latent_ref, query_ref, wh, we, wa, wc, sems,
):
    def chunk(half, first, number, target):
        rows = pl.ds(pl.multiple_of(16 * order_ref[number], 16), 16)
        return pltpu.make_async_copy(
            packed_ref.at[rows, pl.ds(first, 64), :],
            target.at[pl.ds(16 * number, 16)],
            sems.at[half, number],
        )

    copies_e = [chunk(1, 48, i, we) for i in range(TP)]
    copies_h = [chunk(0, 0, i, wh) for i in range(TP)]
    copy_a = pltpu.make_async_copy(packed_ref.at[:, pl.ds(112, 16), :], wa, sems.at[2, 0])
    copy_c = pltpu.make_async_copy(
        packed_ref.at[:, pl.ds(144, 16), pl.ds(0, 256)], wc, sems.at[2, 1]
    )
    for copy in copies_e + copies_h + [copy_a, copy_c]:
        copy.start()
    spread = spread_matrix(F, 14, 16, 1024)
    lane = lax.broadcasted_iota(jnp.int32, (T, 1024), 1) & 63

    def project(blocks, weights, copies, used):
        total = jnp.zeros((T, F), F32)
        squares = jnp.zeros((T, 1), F32)
        for i, ref in enumerate(blocks):
            block = ref[...].astype(F32)
            held = jnp.where(used[:, :128], 0.0, block[:, :128])
            squares = squares + jnp.sum(held, axis=1, keepdims=True)
            block = jnp.where(used, block, 0.0).astype(BF)
            copies[i].wait()
            weight = weights[pl.ds(16 * i, 16)].reshape(1024, F)
            total = total + dot(block, weight)
        return total * lax.rsqrt(squares / D + EPS)

    embed = project((e0, e1, e2, e3), we, copies_e, lane >= 8)
    joined = (project((h0, h1, h2, h3), wh, copies_h, lane < 56) + embed).astype(BF)
    joined_ref[...] = joined
    wide = joined.astype(F32)
    squares = jnp.sum(wide * wide, axis=1, keepdims=True)
    scaled = dot((wide * gain_ref[...]).astype(BF), spread).astype(BF)
    copy_a.wait()
    copy_c.wait()
    down = dot(scaled, wa[...].reshape(1024, F))
    query_ref[...] = down[:, :QL].astype(BF)
    latent_ref[:, :128] = down[:, QL:].astype(BF)
    tail = dot(scaled, wc[...].reshape(1024, 256))
    latent_ref[:, 128:] = (tail + lanes_of(squares, 256, 160)).astype(BF)


def rotate(x, cos_ref, sin_ref):
    first, second = x[: ROPE // 2], x[ROPE // 2 :]
    cosine, sine = cos_ref[...], sin_ref[...]
    return jnp.concatenate(
        [first * cosine - second * sine, first * sine + second * cosine], axis=0
    )


def add_parts(refs):
    a, b, c, d = (ref[...].astype(F32) for ref in refs)
    return (a + b) + (c + d)


def latent_kernel(p0, p1, p2, p3, gl_ref, cos_ref, sin_ref, latent_ref, scale_ref):
    total = add_parts((p0, p1, p2, p3))
    tail = total[:, KL:]
    lane = lax.broadcasted_iota(jnp.int32, tail.shape, 1)
    squares = jnp.sum(
        jnp.where((lane >= 32) & (lane < 35), tail, 0.0), axis=1, keepdims=True
    )
    scale = lax.rsqrt(squares / D + EPS)
    key = total[:, :KL] * scale
    key = key * lax.rsqrt(jnp.mean(key * key, axis=1, keepdims=True) + EPS)
    latent_ref[:KL, :] = jnp.transpose(key * gl_ref[...]).astype(BF)
    rope = rotate(jnp.transpose(tail * scale)[:ROPE], cos_ref, sin_ref)
    latent_ref[KL:, :] = rope.astype(BF)
    scale_ref[...] = jnp.broadcast_to(scale, (T, 128))


def up_kernel(packed_ref, key_ref, value_ref, held, sem):
    copy = pltpu.make_async_copy(packed_ref.at[:, pl.ds(112, 48), :], held, sem)
    copy.start()
    row = lax.broadcasted_iota(jnp.int32, (KL, 1024), 0)
    col = lax.broadcasted_iota(jnp.int32, (KL, 1024), 1) - (row >> 2) * 16
    row = row & 3

    def pick(target):
        return jnp.where(col == target, 1.0, 0.0).astype(BF)

    copy.wait()
    group_a = held[:, 0:16, 0:768].reshape(1024, 768)
    group_b = held[:, 16:32, :].reshape(1024, F)
    group_c = held[:, 32:48, 256:].reshape(1024, 640)
    group_d = held[:, 32:48, :256].reshape(1024, 256)
    spare = pick(12 + row)
    even = pick(jnp.where(row & 1 == 0, 14 + (row >> 1), -9999))
    odd = pick(jnp.where(row & 1 == 1, 14 + (row >> 1), -9999))
    up = jnp.concatenate(
        [
            dot(spare, group_b),
            dot(spare, group_c),
            dot(even, group_a[:, :384]) + dot(odd, group_a[:, 384:]),
            dot(even, group_d[:, :128]) + dot(odd, group_d[:, 128:]),
        ],
        axis=1,
    )
    for head in range(HEADS):
        own = up[:, 128 * head : 128 * head + 128]
        key_ref[:, pl.ds(128 * head, 128)] = own.astype(BF)
        value_ref[pl.ds(VDIM * head, VDIM), :] = jnp.transpose(own)[NOPE:, :].astype(BF)


def query_kernel(
    q0, q1, q2, q3, scale_ref, gq_ref, cos_ref, sin_ref, up_ref, packed_ref, out_ref, held, sem
):
    copy = pltpu.make_async_copy(packed_ref.at[:, pl.ds(128, 32), :], held, sem)
    copy.start()
    spread = spread_matrix(QL, 12, 16, 1024)
    query = add_parts((q0, q1, q2, q3)) * scale_ref[:, :1]
    query = query * lax.rsqrt(jnp.mean(query * query, axis=1, keepdims=True) + EPS)
    query = dot((query * gq_ref[...]).astype(BF), spread).astype(BF)
    copy.wait()
    group_b = held[:, 0:16, :].reshape(1024, F)
    group_c = held[:, 16:32, 256:].reshape(1024, 640)
    projected = jnp.transpose(
        jnp.concatenate([dot(query, group_b), dot(query, group_c)], axis=1)
    )
    scale = (NOPE + ROPE) ** (-0.5) * LOG2E
    width = NOPE + ROPE
    for head in range(HEADS):
        nope = projected[width * head : width * head + NOPE].astype(BF)
        absorbed = dot(up_ref[:, pl.ds(128 * head, NOPE)], nope)
        cols = pl.ds(T * head, T)
        out_ref[:KL, cols] = (absorbed * scale).astype(BF)
        rope = rotate(projected[width * head + NOPE : width * head + width], cos_ref, sin_ref)
        out_ref[KL:, cols] = (rope * scale).astype(BF)


def attend_kernel(chunks, first, last, index_ref, q_ref, *rest):
    held = []
    for _, pieces in chunks:
        held.append(rest[:pieces])
        rest = rest[pieces:]
    if last:
        up_ref, rest = rest[0], rest[1:]
    if not first:
        (m_in, l_in, acc_in), rest = rest[:3], rest[3:]
    if last:
        out_ref, rest = rest[0], rest[1:]
        m_ref, l_ref, acc_ref, keys, values = rest
    else:
        m_ref, l_ref, acc_ref, keys, values = rest
    ep = index_ref[0]
    z, y, core = ep >> 3, (ep >> 1) & 3, ep & 1

    for number, ((dy, dc), _) in enumerate(chunks):
        fresh = first and number == 0
        diagonal = dy == 0 and dc == 0
        for i, block in enumerate(ref[j] for ref in held[number] for j in range(ref.shape[0])):
            keys[pl.ds(T * i, T), :] = jnp.transpose(block)
            values[:, pl.ds(T * i, T)] = block[:KL, :]
        before = ((y - dy) & 3) * 2 + (core ^ dc) <= y * 2 + core
        hidden = [
            jnp.where(dz <= z if dz else before, 0.0, NEGATIVE) for dz in ALONG_Z
        ]

        def step(i):
            cols = pl.ds(i * COLS, COLS)
            scores = dot(keys[...], q_ref[:, cols])
            blocks = [scores[T * i : T * i + T] for i in range(ZS)]
            if diagonal:
                key = lax.broadcasted_iota(jnp.int32, (T, COLS), 0)
                token = lax.broadcasted_iota(jnp.int32, (T, COLS), 1) & (T - 1)
                own = ALONG_Z.index(0)
                blocks[own] = jnp.where(key <= token, blocks[own], NEGATIVE)
            highest = [
                jnp.max(block, axis=0, keepdims=True) + bias
                for block, bias in zip(blocks, hidden)
            ]
            highest = functools.reduce(jnp.maximum, highest)
            if not fresh:
                if first or number > 0:
                    m_old, l_old, acc_old = m_ref[:, cols], l_ref[:, cols], acc_ref[:, cols]
                else:
                    m_old, l_old, acc_old = m_in[:, cols], l_in[:, cols], acc_in[:, cols]
                highest = jnp.maximum(highest, m_old)
                factor = jnp.exp2(m_old - highest)
            weights = [
                jnp.exp2(block - (highest - bias)) for block, bias in zip(blocks, hidden)
            ]
            total = functools.reduce(
                jnp.add, [jnp.sum(w, axis=0, keepdims=True) for w in weights]
            )
            added = dot(
                values[...], jnp.concatenate([w.astype(BF) for w in weights], axis=0)
            )
            if not fresh:
                total = total + l_old * factor
                added = added + acc_old * factor
            m_ref[:, cols] = highest
            l_ref[:, cols] = total
            acc_ref[:, cols] = added

        for i in range(ROWS // COLS):
            step(i)
    if last:
        outs = []
        for head in range(HEADS):
            cols = pl.ds(T * head, T)
            mean = (acc_ref[:, cols] / l_ref[:, cols]).astype(BF)
            outs.append(dot(up_ref[pl.ds(VDIM * head, VDIM), :], mean))
        out_ref[...] = jnp.transpose(jnp.concatenate(outs, axis=0)).astype(BF)


def attend(ep, queries, up, chunks, first, last, state):
    latents = [piece for pieces in chunks.values() for piece in pieces]
    chunks = tuple((place, len(pieces)) for place, pieces in chunks.items())
    carried = [
        jax.ShapeDtypeStruct((1, ROWS), F32),
        jax.ShapeDtypeStruct((1, ROWS), F32),
        jax.ShapeDtypeStruct((KL, ROWS), F32),
    ]
    args = [ep[None], queries, *latents]
    if last:
        args.append(up)
    aliases = {}
    if not first:
        if not last:
            aliases = {len(args) + i: i for i in range(3)}
        args += state
    scratch = [pltpu.VMEM((KEYS, LAT), BF), pltpu.VMEM((KL, KEYS), BF)]
    if last:
        out_shape = [jax.ShapeDtypeStruct((T, HEADS * VDIM), BF)]
        scratch = [pltpu.VMEM(s.shape, F32) for s in carried] + scratch
    else:
        out_shape = carried
    return pl.pallas_call(
        functools.partial(attend_kernel, chunks, first, last),
        out_shape=out_shape,
        in_specs=[pl.BlockSpec(memory_space=pltpu.SMEM)] + [VMEM] * (len(args) - 1),
        out_specs=[VMEM] * len(out_shape),
        scratch_shapes=scratch,
        input_output_aliases=aliases,
        compiler_params=params(32),
        name="attend",
    )(*args)


def ring(x, shift):
    return lax.ppermute(x, "tp", [(i, (i + shift) % TP) for i in range(TP)])


def from_all(x):
    return [x] + [ring(x, shift) for shift in (1, 2, 3)]


def along_z(x, shift):
    return lax.ppermute(x, "ep", [(i, (i + 8 * shift) % EP) for i in range(EP)])


def along_y(x, shift):
    pairs = [(i, (i & ~6) | ((i + 2 * shift) & 6)) for i in range(EP)]
    return lax.ppermute(x, "ep", pairs)


def other_core(x):
    return lax.ppermute(x, "ep", [(i, i ^ 1) for i in range(EP)])


ALONG_Z = (1, 0, 7, 4, 3, 2, 6, 5)


def slot_weights(routes, gates):
    experts = jnp.arange(EXPERTS, dtype=jnp.int32)
    onehot = (routes[:, :, None] == experts[None, None, :]).astype(F32)
    named = jnp.sum(onehot, axis=1)
    earlier = jnp.tril(jnp.ones((T, T), BF), -1)
    before = dot(earlier, named.astype(BF))
    slots = jnp.sum(before[:, None, :] * onehot, axis=2).astype(jnp.int32)
    place = routes * CAP + slots
    lane = jnp.arange(SLOTS, dtype=jnp.int32)
    weights = jnp.zeros((T, SLOTS), F32)
    for k in range(routes.shape[1]):
        weights = weights + jnp.where(place[:, k : k + 1] == lane[None], gates[:, k : k + 1], 0.0)
    return weights


def pack_kernel(hidden_ref, embed_ref, down_ref, query_ref, latent_ref, out_ref):
    hidden, embed, down, query, latent = (
        ref[...].astype(F32) for ref in (hidden_ref, embed_ref, down_ref, query_ref, latent_ref)
    )
    rows = [latent[r : r + 1] for r in range(4)]
    out_ref[pl.ds(0, 112), :] = jnp.concatenate([hidden, embed], axis=0).astype(BF)
    spare = jnp.zeros((1, 128), F32)
    group_1 = jnp.concatenate(
        [
            down[:, :F],
            jnp.concatenate([rows[0][:, 1536:1920], rows[1][:, 1536:1920], spare], axis=1),
            jnp.concatenate([rows[2][:, 1536:1920], rows[3][:, 1536:1920], spare], axis=1),
        ],
        axis=0,
    )
    out_ref[pl.ds(112, 16), :] = group_1.astype(BF)
    group_2 = jnp.concatenate([query[:, :F], latent[:, :F]], axis=0)
    out_ref[pl.ds(128, 16), :] = group_2.astype(BF)
    tail = jnp.concatenate([down[:, F:], jnp.zeros((14, 96), F32)], axis=1)
    left = jnp.concatenate(
        [
            tail,
            jnp.concatenate([rows[0][:, 1920:], rows[1][:, 1920:]], axis=1),
            jnp.concatenate([rows[2][:, 1920:], rows[3][:, 1920:]], axis=1),
        ],
        axis=0,
    )
    right = jnp.concatenate([query[:, F:], latent[:, F:1536]], axis=0)
    out_ref[pl.ds(144, 16), :] = jnp.concatenate([left, right], axis=1).astype(BF)


def split_gates_kernel(weights_ref, hi_ref, lo_ref):
    weights = weights_ref[...]
    hi = weights.astype(BF)
    hi_ref[...] = hi
    lo_ref[...] = (weights - hi.astype(F32)).astype(BF)


def shards(
    hidden_in, next_embed, expert_rows, routes, gates, gain_hidden, gain_embed, join_hidden,
    join_embed, gain_block, down_weight, gain_query, gain_latent, query_up, latent_up,
):
    ep = lax.axis_index("ep")
    tp = lax.axis_index("tp")
    order = jnp.mod(tp - jnp.arange(TP, dtype=jnp.int32), TP)
    order = jnp.concatenate([order, ep[None]])
    smem = pl.BlockSpec(memory_space=pltpu.SMEM)

    packed = lax.all_gather(
        pl.pallas_call(
            pack_kernel,
            out_shape=jax.ShapeDtypeStruct((PACK, F), BF),
            in_specs=[VMEM] * 5,
            out_specs=VMEM,
            name="pack",
        )(join_hidden, join_embed, down_weight, query_up, latent_up),
        "ep",
        axis=0,
        tiled=False,
    )
    received = lax.all_to_all(expert_rows, "ep", split_axis=1, concat_axis=0, tiled=True)
    table = received.reshape(SLOTS, F)

    embeds = from_all(
        pl.pallas_call(
            embed_kernel,
            out_shape=jax.ShapeDtypeStruct((T, 1024), BF),
            in_specs=[VMEM] * 2,
            out_specs=VMEM,
            name="embed",
        )(next_embed, gain_embed[None])
    )
    hi, lo = pl.pallas_call(
        split_gates_kernel,
        out_shape=[jax.ShapeDtypeStruct((T, SLOTS), BF)] * 2,
        in_specs=[VMEM],
        out_specs=[VMEM] * 2,
        name="split_gates",
    )(slot_weights(routes, gates))

    position = (ep * T + jnp.arange(T, dtype=jnp.int32)).astype(F32)
    freq = 10000.0 ** (-jnp.arange(ROPE // 2, dtype=F32) / (ROPE // 2))
    phase = freq[:, None] * position[None, :]
    cosine = jnp.cos(phase)
    sine = jnp.sin(phase)

    hiddens = from_all(
        pl.pallas_call(
            combine_kernel,
            out_shape=jax.ShapeDtypeStruct((T, 1024), BF),
            in_specs=[VMEM] * 5,
            out_specs=VMEM,
            compiler_params=params(32),
            name="combine",
        )(hi, lo, table, hidden_in, gain_hidden[None])
    )
    joined, part, query_part = pl.pallas_call(
        join_kernel,
        out_shape=[
            jax.ShapeDtypeStruct((T, F), BF),
            jax.ShapeDtypeStruct((T, KL + 128), BF),
            jax.ShapeDtypeStruct((T, QL), BF),
        ],
        in_specs=[smem] + [VMEM] * 9 + [HBM],
        out_specs=[VMEM] * 3,
        scratch_shapes=[
            pltpu.VMEM((EP, 64, F), BF),
            pltpu.VMEM((EP, 64, F), BF),
            pltpu.VMEM((EP, 16, F), BF),
            pltpu.VMEM((EP, 16, 256), BF),
            pltpu.SemaphoreType.DMA((3, 4)),
        ],
        compiler_params=params(50),
        name="join",
    )(order, *hiddens, *embeds, gain_block[None], packed)

    latent, scale = pl.pallas_call(
        latent_kernel,
        out_shape=[jax.ShapeDtypeStruct((LAT, T), BF), jax.ShapeDtypeStruct((T, 128), F32)],
        in_specs=[VMEM] * 7,
        out_specs=[VMEM] * 2,
        name="latent",
    )(*from_all(part), gain_latent[None], cosine, sine)
    three = jnp.stack([along_z(latent, 1), latent, along_z(latent, -1)])
    three, later = lax.optimization_barrier((three, packed))
    five = along_z(three, 3), along_z(three[:2], -3)
    three_1, three_3 = along_y(three, 1), along_y(three, -1)
    other_three = other_core(three)
    key_up, value_up = pl.pallas_call(
        up_kernel,
        out_shape=[
            jax.ShapeDtypeStruct((KL, HEADS * 128), BF),
            jax.ShapeDtypeStruct((HEADS * VDIM, KL), BF),
        ],
        in_specs=[HBM],
        out_specs=[VMEM] * 2,
        scratch_shapes=[pltpu.VMEM((EP, 48, F), BF), pltpu.SemaphoreType.DMA],
        compiler_params=params(50),
        name="up",
    )(later)
    queries = pl.pallas_call(
        query_kernel,
        out_shape=jax.ShapeDtypeStruct((LAT, ROWS), BF),
        in_specs=[VMEM] * 9 + [HBM],
        out_specs=VMEM,
        scratch_shapes=[pltpu.VMEM((EP, 32, F), BF), pltpu.SemaphoreType.DMA],
        compiler_params=params(50),
        name="query",
    )(*from_all(query_part), scale, gain_query[None], cosine, sine, key_up, packed)
    five, queries = lax.optimization_barrier((five, queries))
    five = jnp.concatenate(five)
    five_1, five_3 = along_y(five, 1), along_y(five, -1)
    call = functools.partial(attend, ep, queries, value_up)
    state = call(
        {(0, 0): (three, five), (0, 1): (other_three, other_core(five))}, True, False, None
    )
    three_1, three_3, five_1, five_3, state = lax.optimization_barrier(
        (three_1, three_3, five_1, five_3, state)
    )
    chunk_2 = along_y(three_1, 1), along_y(five_3, -1)
    far_1 = other_core(jnp.concatenate([three_1, five_1]))
    far_3 = other_core(jnp.concatenate([three_3, five_3]))
    state = call({(1, 0): (three_1, five_1), (3, 0): (three_3, five_3)}, False, False, state)
    chunk_2, state = lax.optimization_barrier((chunk_2, state))
    far_2 = other_core(jnp.concatenate(chunk_2))
    state = call({(1, 1): (far_1,), (3, 1): (far_3,)}, False, False, state)
    (attended,) = call({(2, 0): chunk_2, (2, 1): (far_2,)}, False, True, state)
    return (joined, attended)


def solution(mesh):
    placed = (
        P("ep", "tp"),
        P("ep", "tp"),
        P("ep", None, None, "tp"),
        P("ep", None),
        P("ep", None),
        P("tp"),
        P("tp"),
        P("ep", "tp"),
        P("ep", "tp"),
        P("tp"),
        P(("tp", "ep"), None),
        P(),
        P(),
        P("ep", "tp"),
        P("ep", "tp"),
    )
    return jax.shard_map(
        shards,
        mesh=mesh,
        in_specs=placed,
        out_specs=(P("ep", "tp"), P("ep", "tp")),
        check_vma=False,
    )
```

```python
import functools

import jax
import jax.numpy as jnp
from jax import lax
from jax.experimental import pallas as pl
from jax.experimental.pallas import tpu as pltpu
from jax.sharding import PartitionSpec as P

D = 3584
NOPE = 64
ROPE = 32
VDIM = 64
QL = 768
KL = 256
EPS = 1e-06
NEGATIVE = -1e30
LOG2E = 1.4426950408889634

T = 128
F = 896
HEADS = 16
EP = 64
TP = 4
CAP = 8
EXPERTS = 256
SLOTS = EXPERTS * CAP
PACK = 160
LAT = KL + ROPE
ROWS = HEADS * T
COLS = 1024

BF = jnp.bfloat16
F32 = jnp.float32
VMEM = pl.BlockSpec(memory_space=pltpu.VMEM)
HBM = pl.BlockSpec(memory_space=pltpu.HBM)
MIB = 1 << 20


def params(mib):
    return pltpu.CompilerParams(vmem_limit_bytes=mib * MIB)


def dot(a, b):
    return jnp.dot(a, b, preferred_element_type=F32)


def dot_nt(a, b):
    return lax.dot_general(a, b, (((1,), (1,)), ((), ())), preferred_element_type=F32)


def split3(s):
    hi = s.astype(BF).astype(F32)
    mid = (s - hi).astype(BF).astype(F32)
    low = (s - hi - mid).astype(BF).astype(F32)
    return hi, mid, low


def lanes_of(s, width, first):
    hi, mid, low = split3(s)
    lane = lax.broadcasted_iota(jnp.int32, (s.shape[0], width), 1)
    return jnp.where(
        lane == first,
        hi,
        jnp.where(lane == first + 1, mid, jnp.where(lane == first + 2, low, 0.0)),
    )


def spread_matrix(rows, used, width, cols, skip=0):
    row = lax.broadcasted_iota(jnp.int32, (rows, cols), 0)
    col = lax.broadcasted_iota(jnp.int32, (rows, cols), 1)
    part = (col & (width - 1)) - skip
    target = jnp.where(
        (part >= 0) & (part < used), (col >> (width.bit_length() - 1)) * used + part, -1
    )
    return jnp.where(row == target, 1.0, 0.0).astype(BF)


def features_store(out_ref, state, gain, skip):
    spread = spread_matrix(F, 56, 64, 1024, skip)
    squares = jnp.sum(state * state, axis=1, keepdims=True)
    scaled = dot((state * gain).astype(BF), spread)
    lanes = lanes_of(squares, 128, 0 if skip else 56)
    out_ref[:, :128] = (scaled[:, :128] + lanes).astype(BF)
    out_ref[:, 128:] = scaled[:, 128:].astype(BF)


def embed_kernel(embed_ref, gain_ref, out_ref):
    features_store(out_ref, embed_ref[...].astype(F32), gain_ref[...], 8)


def combine_kernel(hi_ref, lo_ref, table_ref, hidden_ref, gain_ref, out_ref):
    moe = dot(hi_ref[...], table_ref[...]) + dot(lo_ref[...], table_ref[...])
    features_store(out_ref, hidden_ref[...].astype(F32) + moe, gain_ref[...], 0)


def join_kernel(
    order_ref, h0, h1, h2, h3, e0, e1, e2, e3, gain_ref, packed_ref,
    joined_ref, latent_ref, query_ref, wh, we, wa, wc, sems,
):
    def chunk(half, first, number, target):
        rows = pl.ds(pl.multiple_of(16 * order_ref[number], 16), 16)
        return pltpu.make_async_copy(
            packed_ref.at[rows, pl.ds(first, 64), :],
            target.at[pl.ds(16 * number, 16)],
            sems.at[half, number],
        )

    copies_e = [chunk(1, 48, i, we) for i in range(TP)]
    copies_h = [chunk(0, 0, i, wh) for i in range(TP)]
    copy_a = pltpu.make_async_copy(packed_ref.at[:, pl.ds(112, 16), :], wa, sems.at[2, 0])
    copy_c = pltpu.make_async_copy(
        packed_ref.at[:, pl.ds(144, 16), pl.ds(0, 256)], wc, sems.at[2, 1]
    )
    for copy in copies_e + copies_h + [copy_a, copy_c]:
        copy.start()
    spread = spread_matrix(F, 14, 16, 1024)
    lane = lax.broadcasted_iota(jnp.int32, (T, 1024), 1) & 63

    def project(blocks, weights, copies, used):
        total = jnp.zeros((T, F), F32)
        squares = jnp.zeros((T, 1), F32)
        for i, ref in enumerate(blocks):
            block = ref[...].astype(F32)
            held = jnp.where(used[:, :128], 0.0, block[:, :128])
            squares = squares + jnp.sum(held, axis=1, keepdims=True)
            block = jnp.where(used, block, 0.0).astype(BF)
            copies[i].wait()
            weight = weights[pl.ds(16 * i, 16)].reshape(1024, F)
            total = total + dot(block, weight)
        return total * lax.rsqrt(squares / D + EPS)

    embed = project((e0, e1, e2, e3), we, copies_e, lane >= 8)
    joined = (project((h0, h1, h2, h3), wh, copies_h, lane < 56) + embed).astype(BF)
    joined_ref[...] = joined
    wide = joined.astype(F32)
    squares = jnp.sum(wide * wide, axis=1, keepdims=True)
    scaled = dot((wide * gain_ref[...]).astype(BF), spread).astype(BF)
    copy_a.wait()
    copy_c.wait()
    down = dot(scaled, wa[...].reshape(1024, F))
    query_ref[...] = down[:, :QL].astype(BF)
    latent_ref[:, :128] = down[:, QL:].astype(BF)
    tail = dot(scaled, wc[...].reshape(1024, 256))
    latent_ref[:, 128:] = (tail + lanes_of(squares, 256, 160)).astype(BF)


def rotate(x, cos_ref, sin_ref):
    first, second = x[: ROPE // 2], x[ROPE // 2 :]
    cosine, sine = cos_ref[...], sin_ref[...]
    return jnp.concatenate(
        [first * cosine - second * sine, first * sine + second * cosine], axis=0
    )


def add_parts(refs):
    a, b, c, d = (ref[...].astype(F32) for ref in refs)
    return (a + b) + (c + d)


def latent_kernel(p0, p1, p2, p3, gl_ref, cos_ref, sin_ref, latent_ref, scale_ref):
    total = add_parts((p0, p1, p2, p3))
    tail = total[:, KL:]
    lane = lax.broadcasted_iota(jnp.int32, tail.shape, 1)
    squares = jnp.sum(
        jnp.where((lane >= 32) & (lane < 35), tail, 0.0), axis=1, keepdims=True
    )
    scale = lax.rsqrt(squares / D + EPS)
    key = total[:, :KL] * scale
    key = key * lax.rsqrt(jnp.mean(key * key, axis=1, keepdims=True) + EPS)
    latent_ref[:KL, :] = jnp.transpose(key * gl_ref[...]).astype(BF)
    rope = rotate(jnp.transpose(tail * scale)[:ROPE], cos_ref, sin_ref)
    latent_ref[KL:, :] = rope.astype(BF)
    scale_ref[...] = jnp.broadcast_to(scale, (T, 128))


def up_kernel(packed_ref, key_ref, value_ref, held, sem):
    copy = pltpu.make_async_copy(packed_ref.at[:, pl.ds(112, 48), :], held, sem)
    copy.start()
    row = lax.broadcasted_iota(jnp.int32, (KL, 1024), 0)
    col = lax.broadcasted_iota(jnp.int32, (KL, 1024), 1) - (row >> 2) * 16
    row = row & 3

    def pick(target):
        return jnp.where(col == target, 1.0, 0.0).astype(BF)

    copy.wait()
    group_a = held[:, 0:16, 0:768].reshape(1024, 768)
    group_b = held[:, 16:32, :].reshape(1024, F)
    group_c = held[:, 32:48, 256:].reshape(1024, 640)
    group_d = held[:, 32:48, :256].reshape(1024, 256)
    spare = pick(12 + row)
    even = pick(jnp.where(row & 1 == 0, 14 + (row >> 1), -9999))
    odd = pick(jnp.where(row & 1 == 1, 14 + (row >> 1), -9999))
    up = jnp.concatenate(
        [
            dot(spare, group_b),
            dot(spare, group_c),
            dot(even, group_a[:, :384]) + dot(odd, group_a[:, 384:]),
            dot(even, group_d[:, :128]) + dot(odd, group_d[:, 128:]),
        ],
        axis=1,
    )
    for head in range(HEADS):
        own = up[:, 128 * head : 128 * head + 128]
        key_ref[:, pl.ds(128 * head, 128)] = own.astype(BF)
        value_ref[pl.ds(VDIM * head, VDIM), :] = jnp.transpose(own)[NOPE:, :].astype(BF)


def query_kernel(
    q0, q1, q2, q3, scale_ref, gq_ref, cos_ref, sin_ref, up_ref, packed_ref, out_ref, held, sem
):
    copy = pltpu.make_async_copy(packed_ref.at[:, pl.ds(128, 32), :], held, sem)
    copy.start()
    spread = spread_matrix(QL, 12, 16, 1024)
    query = add_parts((q0, q1, q2, q3)) * scale_ref[:, :1]
    query = query * lax.rsqrt(jnp.mean(query * query, axis=1, keepdims=True) + EPS)
    query = dot((query * gq_ref[...]).astype(BF), spread).astype(BF)
    copy.wait()
    group_b = held[:, 0:16, :].reshape(1024, F)
    group_c = held[:, 16:32, 256:].reshape(1024, 640)
    projected = jnp.transpose(
        jnp.concatenate([dot(query, group_b), dot(query, group_c)], axis=1)
    )
    scale = (NOPE + ROPE) ** (-0.5) * LOG2E
    width = NOPE + ROPE
    for head in range(HEADS):
        nope = projected[width * head : width * head + NOPE].astype(BF)
        absorbed = dot(up_ref[:, pl.ds(128 * head, NOPE)], nope)
        cols = pl.ds(T * head, T)
        out_ref[:KL, cols] = (absorbed * scale).astype(BF)
        rope = rotate(projected[width * head + NOPE : width * head + width], cos_ref, sin_ref)
        out_ref[KL:, cols] = (rope * scale).astype(BF)


def attend_kernel(groups, first, last, index_ref, q_ref, *rest):
    held = []
    for group in groups:
        held.append(rest[: len(group)])
        rest = rest[len(group) :]
    if last:
        up_ref, rest = rest[0], rest[1:]
    if not first:
        (m_in, l_in, acc_in), rest = rest[:3], rest[3:]
    if last:
        out_ref, rest = rest[0], rest[1:]
        m_ref, l_ref, acc_ref, keys, values = rest
    else:
        m_ref, l_ref, acc_ref, keys, values = rest
    ep = index_ref[0]
    z, y, core = ep >> 3, (ep >> 1) & 3, ep & 1

    for number, group in enumerate(groups):
        fresh = first and number == 0
        diagonal, hidden = None, []
        for (place, places_z), ref in zip(group, held[number]):
            dy, dc = place
            before = ((y - dy) & 3) * 2 + (core ^ dc) <= y * 2 + core
            for j, dz in enumerate(places_z):
                i = len(hidden)
                keys[pl.ds(T * i, T), :] = jnp.transpose(ref[j])
                values[:, pl.ds(T * i, T)] = ref[j, :KL, :]
                if place == (0, 0) and dz == 0:
                    diagonal = i
                hidden.append(jnp.where(dz <= z if dz else before, 0.0, NEGATIVE))
        span = T * len(hidden)

        def step(i):
            cols = pl.ds(i * COLS, COLS)
            scores = dot(keys[:span, :], q_ref[:, cols])
            blocks = [scores[T * j : T * j + T] for j in range(len(hidden))]
            if diagonal is not None:
                key = lax.broadcasted_iota(jnp.int32, (T, COLS), 0)
                token = lax.broadcasted_iota(jnp.int32, (T, COLS), 1) & (T - 1)
                blocks[diagonal] = jnp.where(key <= token, blocks[diagonal], NEGATIVE)
            highest = [
                jnp.max(block, axis=0, keepdims=True) + bias
                for block, bias in zip(blocks, hidden)
            ]
            highest = functools.reduce(jnp.maximum, highest)
            if not fresh:
                if first or number > 0:
                    m_old, l_old, acc_old = m_ref[:, cols], l_ref[:, cols], acc_ref[:, cols]
                else:
                    m_old, l_old, acc_old = m_in[:, cols], l_in[:, cols], acc_in[:, cols]
                highest = jnp.maximum(highest, m_old)
                factor = jnp.exp2(m_old - highest)
            weights = [
                jnp.exp2(block - (highest - bias)) for block, bias in zip(blocks, hidden)
            ]
            total = functools.reduce(
                jnp.add, [jnp.sum(w, axis=0, keepdims=True) for w in weights]
            )
            added = dot(
                values[:, :span], jnp.concatenate([w.astype(BF) for w in weights], axis=0)
            )
            if not fresh:
                total = total + l_old * factor
                added = added + acc_old * factor
            m_ref[:, cols] = highest
            l_ref[:, cols] = total
            acc_ref[:, cols] = added

        for i in range(ROWS // COLS):
            step(i)
    if last:
        outs = []
        for head in range(HEADS):
            cols = pl.ds(T * head, T)
            mean = (acc_ref[:, cols] / l_ref[:, cols]).astype(BF)
            outs.append(dot(up_ref[pl.ds(VDIM * head, VDIM), :], mean))
        out_ref[...] = jnp.transpose(jnp.concatenate(outs, axis=0)).astype(BF)


def attend(ep, queries, up, groups, first, last, state):
    latents = [array for group in groups for _, _, array in group]
    groups = tuple(tuple((place, dz) for place, dz, _ in group) for group in groups)
    blocks = max(sum(len(dz) for _, dz in group) for group in groups)
    carried = [
        jax.ShapeDtypeStruct((1, ROWS), F32),
        jax.ShapeDtypeStruct((1, ROWS), F32),
        jax.ShapeDtypeStruct((KL, ROWS), F32),
    ]
    args = [ep[None], queries, *latents]
    if last:
        args.append(up)
    aliases = {}
    if not first:
        if not last:
            aliases = {len(args) + i: i for i in range(3)}
        args += state
    scratch = [pltpu.VMEM((T * blocks, LAT), BF), pltpu.VMEM((KL, T * blocks), BF)]
    if last:
        out_shape = [jax.ShapeDtypeStruct((T, HEADS * VDIM), BF)]
        scratch = [pltpu.VMEM(s.shape, F32) for s in carried] + scratch
    else:
        out_shape = carried
    return pl.pallas_call(
        functools.partial(attend_kernel, groups, first, last),
        out_shape=out_shape,
        in_specs=[pl.BlockSpec(memory_space=pltpu.SMEM)] + [VMEM] * (len(args) - 1),
        out_specs=[VMEM] * len(out_shape),
        scratch_shapes=scratch,
        input_output_aliases=aliases,
        compiler_params=params(32),
        name="attend",
    )(*args)


def ring(x, shift):
    return lax.ppermute(x, "tp", [(i, (i + shift) % TP) for i in range(TP)])


def from_all(x):
    return [x] + [ring(x, shift) for shift in (1, 2, 3)]


def along_z(x, shift):
    return lax.ppermute(x, "ep", [(i, (i + 8 * shift) % EP) for i in range(EP)])


def along_y(x, shift):
    pairs = [(i, (i & ~6) | ((i + 2 * shift) & 6)) for i in range(EP)]
    return lax.ppermute(x, "ep", pairs)


def other_core(x):
    return lax.ppermute(x, "ep", [(i, i ^ 1) for i in range(EP)])


THREE = (1, 0, 7)
FIVE = (4, 3, 2, 6, 5)
EIGHT = THREE + FIVE


def slot_weights(routes, gates):
    experts = jnp.arange(EXPERTS, dtype=jnp.int32)
    onehot = (routes[:, :, None] == experts[None, None, :]).astype(F32)
    named = jnp.sum(onehot, axis=1)
    earlier = jnp.tril(jnp.ones((T, T), BF), -1)
    before = dot(earlier, named.astype(BF))
    slots = jnp.sum(before[:, None, :] * onehot, axis=2).astype(jnp.int32)
    place = routes * CAP + slots
    lane = jnp.arange(SLOTS, dtype=jnp.int32)
    weights = jnp.zeros((T, SLOTS), F32)
    for k in range(routes.shape[1]):
        weights = weights + jnp.where(place[:, k : k + 1] == lane[None], gates[:, k : k + 1], 0.0)
    return weights


def pack_kernel(hidden_ref, embed_ref, down_ref, query_ref, latent_ref, out_ref):
    hidden, embed, down, query, latent = (
        ref[...].astype(F32) for ref in (hidden_ref, embed_ref, down_ref, query_ref, latent_ref)
    )
    rows = [latent[r : r + 1] for r in range(4)]
    out_ref[pl.ds(0, 112), :] = jnp.concatenate([hidden, embed], axis=0).astype(BF)
    spare = jnp.zeros((1, 128), F32)
    group_1 = jnp.concatenate(
        [
            down[:, :F],
            jnp.concatenate([rows[0][:, 1536:1920], rows[1][:, 1536:1920], spare], axis=1),
            jnp.concatenate([rows[2][:, 1536:1920], rows[3][:, 1536:1920], spare], axis=1),
        ],
        axis=0,
    )
    out_ref[pl.ds(112, 16), :] = group_1.astype(BF)
    group_2 = jnp.concatenate([query[:, :F], latent[:, :F]], axis=0)
    out_ref[pl.ds(128, 16), :] = group_2.astype(BF)
    tail = jnp.concatenate([down[:, F:], jnp.zeros((14, 96), F32)], axis=1)
    left = jnp.concatenate(
        [
            tail,
            jnp.concatenate([rows[0][:, 1920:], rows[1][:, 1920:]], axis=1),
            jnp.concatenate([rows[2][:, 1920:], rows[3][:, 1920:]], axis=1),
        ],
        axis=0,
    )
    right = jnp.concatenate([query[:, F:], latent[:, F:1536]], axis=0)
    out_ref[pl.ds(144, 16), :] = jnp.concatenate([left, right], axis=1).astype(BF)


def split_gates_kernel(weights_ref, hi_ref, lo_ref):
    weights = weights_ref[...]
    hi = weights.astype(BF)
    hi_ref[...] = hi
    lo_ref[...] = (weights - hi.astype(F32)).astype(BF)


def shards(
    hidden_in, next_embed, expert_rows, routes, gates, gain_hidden, gain_embed, join_hidden,
    join_embed, gain_block, down_weight, gain_query, gain_latent, query_up, latent_up,
):
    ep = lax.axis_index("ep")
    tp = lax.axis_index("tp")
    order = jnp.mod(tp - jnp.arange(TP, dtype=jnp.int32), TP)
    order = jnp.concatenate([order, ep[None]])
    smem = pl.BlockSpec(memory_space=pltpu.SMEM)

    packed = lax.all_gather(
        pl.pallas_call(
            pack_kernel,
            out_shape=jax.ShapeDtypeStruct((PACK, F), BF),
            in_specs=[VMEM] * 5,
            out_specs=VMEM,
            name="pack",
        )(join_hidden, join_embed, down_weight, query_up, latent_up),
        "ep",
        axis=0,
        tiled=False,
    )
    received = lax.all_to_all(expert_rows, "ep", split_axis=1, concat_axis=0, tiled=True)
    table = received.reshape(SLOTS, F)

    embeds = from_all(
        pl.pallas_call(
            embed_kernel,
            out_shape=jax.ShapeDtypeStruct((T, 1024), BF),
            in_specs=[VMEM] * 2,
            out_specs=VMEM,
            name="embed",
        )(next_embed, gain_embed[None])
    )
    hi, lo = pl.pallas_call(
        split_gates_kernel,
        out_shape=[jax.ShapeDtypeStruct((T, SLOTS), BF)] * 2,
        in_specs=[VMEM],
        out_specs=[VMEM] * 2,
        name="split_gates",
    )(slot_weights(routes, gates))

    position = (ep * T + jnp.arange(T, dtype=jnp.int32)).astype(F32)
    freq = 10000.0 ** (-jnp.arange(ROPE // 2, dtype=F32) / (ROPE // 2))
    phase = freq[:, None] * position[None, :]
    cosine = jnp.cos(phase)
    sine = jnp.sin(phase)

    hiddens = from_all(
        pl.pallas_call(
            combine_kernel,
            out_shape=jax.ShapeDtypeStruct((T, 1024), BF),
            in_specs=[VMEM] * 5,
            out_specs=VMEM,
            compiler_params=params(32),
            name="combine",
        )(hi, lo, table, hidden_in, gain_hidden[None])
    )
    joined, part, query_part = pl.pallas_call(
        join_kernel,
        out_shape=[
            jax.ShapeDtypeStruct((T, F), BF),
            jax.ShapeDtypeStruct((T, KL + 128), BF),
            jax.ShapeDtypeStruct((T, QL), BF),
        ],
        in_specs=[smem] + [VMEM] * 9 + [HBM],
        out_specs=[VMEM] * 3,
        scratch_shapes=[
            pltpu.VMEM((EP, 64, F), BF),
            pltpu.VMEM((EP, 64, F), BF),
            pltpu.VMEM((EP, 16, F), BF),
            pltpu.VMEM((EP, 16, 256), BF),
            pltpu.SemaphoreType.DMA((3, 4)),
        ],
        compiler_params=params(50),
        name="join",
    )(order, *hiddens, *embeds, gain_block[None], packed)

    latent, scale = pl.pallas_call(
        latent_kernel,
        out_shape=[jax.ShapeDtypeStruct((LAT, T), BF), jax.ShapeDtypeStruct((T, 128), F32)],
        in_specs=[VMEM] * 7,
        out_specs=[VMEM] * 2,
        name="latent",
    )(*from_all(part), gain_latent[None], cosine, sine)
    latent, later = lax.optimization_barrier((latent, packed))
    three = jnp.stack([along_z(latent, 1), latent, along_z(latent, -1)])
    three, query_part = lax.optimization_barrier((three, query_part))
    five = along_z(three, 3), along_z(three[:2], -3)
    three_1, three_3 = along_y(three, 1), along_y(three, -1)
    other_three = other_core(three)
    key_up, value_up = pl.pallas_call(
        up_kernel,
        out_shape=[
            jax.ShapeDtypeStruct((KL, HEADS * 128), BF),
            jax.ShapeDtypeStruct((HEADS * VDIM, KL), BF),
        ],
        in_specs=[HBM],
        out_specs=[VMEM] * 2,
        scratch_shapes=[pltpu.VMEM((EP, 48, F), BF), pltpu.SemaphoreType.DMA],
        compiler_params=params(50),
        name="up",
    )(later)
    three_1, three_3, other_three, key_up = lax.optimization_barrier(
        (three_1, three_3, other_three, key_up)
    )
    queries = pl.pallas_call(
        query_kernel,
        out_shape=jax.ShapeDtypeStruct((LAT, ROWS), BF),
        in_specs=[VMEM] * 9 + [HBM],
        out_specs=VMEM,
        scratch_shapes=[pltpu.VMEM((EP, 32, F), BF), pltpu.SemaphoreType.DMA],
        compiler_params=params(50),
        name="query",
    )(*from_all(query_part), scale, gain_query[None], cosine, sine, key_up, packed)
    five, queries = lax.optimization_barrier((five, queries))
    five = jnp.concatenate(five)
    five_1, five_3 = along_y(five, 1), along_y(five, -1)
    call = functools.partial(attend, ep, queries, value_up)
    state = call(
        [
            [((0, 0), THREE, three), ((0, 0), FIVE, five)],
            [((0, 1), THREE, other_three), ((0, 1), FIVE, other_core(five))],
            [((1, 0), THREE, three_1), ((3, 0), THREE, three_3)],
        ],
        True,
        False,
        None,
    )
    three_1, three_3, five_1, five_3, state = lax.optimization_barrier(
        (three_1, three_3, five_1, five_3, state)
    )
    chunk_2 = along_y(three_1, 1), along_y(five_3, -1)
    far_1 = other_core(jnp.concatenate([three_1, five_1]))
    far_3 = other_core(jnp.concatenate([three_3, five_3]))
    state = call([[((1, 0), FIVE, five_1), ((3, 0), FIVE, five_3)]], False, False, state)
    chunk_2, state = lax.optimization_barrier((chunk_2, state))
    far_2 = other_core(jnp.concatenate(chunk_2))
    state = call([[((1, 1), EIGHT, far_1)], [((3, 1), EIGHT, far_3)]], False, False, state)
    (attended,) = call(
        [
            [((2, 0), THREE, chunk_2[0]), ((2, 0), FIVE, chunk_2[1])],
            [((2, 1), EIGHT, far_2)],
        ],
        False,
        True,
        state,
    )
    return (joined, attended)


def solution(mesh):
    placed = (
        P("ep", "tp"),
        P("ep", "tp"),
        P("ep", None, None, "tp"),
        P("ep", None),
        P("ep", None),
        P("tp"),
        P("tp"),
        P("ep", "tp"),
        P("ep", "tp"),
        P("tp"),
        P(("tp", "ep"), None),
        P(),
        P(),
        P("ep", "tp"),
        P("ep", "tp"),
    )
    return jax.shard_map(
        shards,
        mesh=mesh,
        in_specs=placed,
        out_specs=(P("ep", "tp"), P("ep", "tp")),
        check_vma=False,
    )
```

```python
import functools

import jax
import jax.numpy as jnp
from jax import lax
from jax.experimental import pallas as pl
from jax.experimental.pallas import tpu as pltpu
from jax.sharding import PartitionSpec as P

D = 3584
NOPE = 64
ROPE = 32
VDIM = 64
QL = 768
KL = 256
EPS = 1e-06
NEGATIVE = -1e30
LOG2E = 1.4426950408889634

T = 128
F = 896
HEADS = 16
EP = 64
TP = 4
CAP = 8
EXPERTS = 256
SLOTS = EXPERTS * CAP
PACK = 160
LAT = KL + ROPE
ROWS = HEADS * T
COLS = 1024

BF = jnp.bfloat16
F32 = jnp.float32
VMEM = pl.BlockSpec(memory_space=pltpu.VMEM)
HBM = pl.BlockSpec(memory_space=pltpu.HBM)
MIB = 1 << 20


def params(mib):
    return pltpu.CompilerParams(vmem_limit_bytes=mib * MIB)


def dot(a, b):
    return jnp.dot(a, b, preferred_element_type=F32)


def dot_nt(a, b):
    return lax.dot_general(a, b, (((1,), (1,)), ((), ())), preferred_element_type=F32)


def split3(s):
    hi = s.astype(BF).astype(F32)
    mid = (s - hi).astype(BF).astype(F32)
    low = (s - hi - mid).astype(BF).astype(F32)
    return hi, mid, low


def lanes_of(s, width, first):
    hi, mid, low = split3(s)
    lane = lax.broadcasted_iota(jnp.int32, (s.shape[0], width), 1)
    return jnp.where(
        lane == first,
        hi,
        jnp.where(lane == first + 1, mid, jnp.where(lane == first + 2, low, 0.0)),
    )


def spread_matrix(rows, used, width, cols, skip=0):
    row = lax.broadcasted_iota(jnp.int32, (rows, cols), 0)
    col = lax.broadcasted_iota(jnp.int32, (rows, cols), 1)
    part = (col & (width - 1)) - skip
    target = jnp.where(
        (part >= 0) & (part < used), (col >> (width.bit_length() - 1)) * used + part, -1
    )
    return jnp.where(row == target, 1.0, 0.0).astype(BF)


def features_store(out_ref, state, gain, skip):
    spread = spread_matrix(F, 56, 64, 1024, skip)
    squares = jnp.sum(state * state, axis=1, keepdims=True)
    scaled = dot((state * gain).astype(BF), spread)
    lanes = lanes_of(squares, 128, 0 if skip else 56)
    out_ref[:, :128] = (scaled[:, :128] + lanes).astype(BF)
    out_ref[:, 128:] = scaled[:, 128:].astype(BF)


def embed_kernel(embed_ref, gain_ref, out_ref):
    features_store(out_ref, embed_ref[...].astype(F32), gain_ref[...], 8)


def combine_kernel(hi_ref, lo_ref, table_ref, hidden_ref, gain_ref, out_ref):
    moe = dot(hi_ref[...], table_ref[...]) + dot(lo_ref[...], table_ref[...])
    features_store(out_ref, hidden_ref[...].astype(F32) + moe, gain_ref[...], 0)


def join_kernel(
    order_ref, h0, h1, h2, h3, e0, e1, e2, e3, gain_ref, packed_ref,
    joined_ref, latent_ref, query_ref, wh, we, wa, wc, sems,
):
    def chunk(half, first, number, target):
        rows = pl.ds(pl.multiple_of(16 * order_ref[number], 16), 16)
        return pltpu.make_async_copy(
            packed_ref.at[rows, pl.ds(first, 64), :],
            target.at[pl.ds(16 * number, 16)],
            sems.at[half, number],
        )

    copies_e = [chunk(1, 48, i, we) for i in range(TP)]
    copies_h = [chunk(0, 0, i, wh) for i in range(TP)]
    copy_a = pltpu.make_async_copy(packed_ref.at[:, pl.ds(112, 16), :], wa, sems.at[2, 0])
    copy_c = pltpu.make_async_copy(
        packed_ref.at[:, pl.ds(144, 16), pl.ds(0, 256)], wc, sems.at[2, 1]
    )
    for copy in copies_e + copies_h + [copy_a, copy_c]:
        copy.start()
    spread = spread_matrix(F, 14, 16, 1024)
    lane = lax.broadcasted_iota(jnp.int32, (T, 1024), 1) & 63

    def project(blocks, weights, copies, used):
        total = jnp.zeros((T, F), F32)
        squares = jnp.zeros((T, 1), F32)
        for i, ref in enumerate(blocks):
            block = ref[...].astype(F32)
            held = jnp.where(used[:, :128], 0.0, block[:, :128])
            squares = squares + jnp.sum(held, axis=1, keepdims=True)
            block = jnp.where(used, block, 0.0).astype(BF)
            copies[i].wait()
            weight = weights[pl.ds(16 * i, 16)].reshape(1024, F)
            total = total + dot(block, weight)
        return total * lax.rsqrt(squares / D + EPS)

    embed = project((e0, e1, e2, e3), we, copies_e, lane >= 8)
    joined = (project((h0, h1, h2, h3), wh, copies_h, lane < 56) + embed).astype(BF)
    joined_ref[...] = joined
    wide = joined.astype(F32)
    squares = jnp.sum(wide * wide, axis=1, keepdims=True)
    scaled = dot((wide * gain_ref[...]).astype(BF), spread).astype(BF)
    copy_a.wait()
    copy_c.wait()
    down = dot(scaled, wa[...].reshape(1024, F))
    query_ref[...] = down[:, :QL].astype(BF)
    latent_ref[:, :128] = down[:, QL:].astype(BF)
    tail = dot(scaled, wc[...].reshape(1024, 256))
    latent_ref[:, 128:] = (tail + lanes_of(squares, 256, 160)).astype(BF)


def rotate(x, cos_ref, sin_ref):
    first, second = x[: ROPE // 2], x[ROPE // 2 :]
    cosine, sine = cos_ref[...], sin_ref[...]
    return jnp.concatenate(
        [first * cosine - second * sine, first * sine + second * cosine], axis=0
    )


def add_parts(refs):
    a, b, c, d = (ref[...].astype(F32) for ref in refs)
    return (a + b) + (c + d)


def latent_kernel(p0, p1, p2, p3, gl_ref, cos_ref, sin_ref, latent_ref, scale_ref):
    total = add_parts((p0, p1, p2, p3))
    tail = total[:, KL:]
    lane = lax.broadcasted_iota(jnp.int32, tail.shape, 1)
    squares = jnp.sum(
        jnp.where((lane >= 32) & (lane < 35), tail, 0.0), axis=1, keepdims=True
    )
    scale = lax.rsqrt(squares / D + EPS)
    key = total[:, :KL] * scale
    key = key * lax.rsqrt(jnp.mean(key * key, axis=1, keepdims=True) + EPS)
    latent_ref[:KL, :] = jnp.transpose(key * gl_ref[...]).astype(BF)
    rope = rotate(jnp.transpose(tail * scale)[:ROPE], cos_ref, sin_ref)
    latent_ref[KL:, :] = rope.astype(BF)
    scale_ref[...] = jnp.broadcast_to(scale, (T, 128))


def up_kernel(packed_ref, key_ref, value_ref, held, sem):
    copy = pltpu.make_async_copy(packed_ref.at[:, pl.ds(112, 48), :], held, sem)
    copy.start()
    row = lax.broadcasted_iota(jnp.int32, (KL, 1024), 0)
    col = lax.broadcasted_iota(jnp.int32, (KL, 1024), 1) - (row >> 2) * 16
    row = row & 3

    def pick(target):
        return jnp.where(col == target, 1.0, 0.0).astype(BF)

    copy.wait()
    group_a = held[:, 0:16, 0:768].reshape(1024, 768)
    group_b = held[:, 16:32, :].reshape(1024, F)
    group_c = held[:, 32:48, 256:].reshape(1024, 640)
    group_d = held[:, 32:48, :256].reshape(1024, 256)
    spare = pick(12 + row)
    even = pick(jnp.where(row & 1 == 0, 14 + (row >> 1), -9999))
    odd = pick(jnp.where(row & 1 == 1, 14 + (row >> 1), -9999))
    up = jnp.concatenate(
        [
            dot(spare, group_b),
            dot(spare, group_c),
            dot(even, group_a[:, :384]) + dot(odd, group_a[:, 384:]),
            dot(even, group_d[:, :128]) + dot(odd, group_d[:, 128:]),
        ],
        axis=1,
    )
    for head in range(HEADS):
        own = up[:, 128 * head : 128 * head + 128]
        key_ref[:, pl.ds(128 * head, 128)] = own.astype(BF)
        value_ref[pl.ds(VDIM * head, VDIM), :] = jnp.transpose(own)[NOPE:, :].astype(BF)


def query_kernel(
    q0, q1, q2, q3, scale_ref, gq_ref, cos_ref, sin_ref, up_ref, packed_ref, out_ref, held, sem
):
    copy = pltpu.make_async_copy(packed_ref.at[:, pl.ds(128, 32), :], held, sem)
    copy.start()
    spread = spread_matrix(QL, 12, 16, 1024)
    query = add_parts((q0, q1, q2, q3)) * scale_ref[:, :1]
    query = query * lax.rsqrt(jnp.mean(query * query, axis=1, keepdims=True) + EPS)
    query = dot((query * gq_ref[...]).astype(BF), spread).astype(BF)
    copy.wait()
    group_b = held[:, 0:16, :].reshape(1024, F)
    group_c = held[:, 16:32, 256:].reshape(1024, 640)
    projected = jnp.transpose(
        jnp.concatenate([dot(query, group_b), dot(query, group_c)], axis=1)
    )
    scale = (NOPE + ROPE) ** (-0.5) * LOG2E
    width = NOPE + ROPE
    for head in range(HEADS):
        nope = projected[width * head : width * head + NOPE].astype(BF)
        absorbed = dot(up_ref[:, pl.ds(128 * head, NOPE)], nope)
        cols = pl.ds(T * head, T)
        out_ref[:KL, cols] = (absorbed * scale).astype(BF)
        rope = rotate(projected[width * head + NOPE : width * head + width], cos_ref, sin_ref)
        out_ref[KL:, cols] = (rope * scale).astype(BF)


def attend_kernel(groups, first, last, index_ref, q_ref, *rest):
    held = []
    for group in groups:
        held.append(rest[: len(group)])
        rest = rest[len(group) :]
    if last:
        up_ref, rest = rest[0], rest[1:]
    if not first:
        (m_in, l_in, acc_in), rest = rest[:3], rest[3:]
    if last:
        out_ref, rest = rest[0], rest[1:]
        m_ref, l_ref, acc_ref, keys, values = rest
    else:
        m_ref, l_ref, acc_ref, keys, values = rest
    ep = index_ref[0]
    z, y, core = ep >> 3, (ep >> 1) & 3, ep & 1

    for number, group in enumerate(groups):
        fresh = first and number == 0
        diagonal, hidden = None, []
        for (place, places_z), ref in zip(group, held[number]):
            dy, dc = place
            before = ((y - dy) & 3) * 2 + (core ^ dc) <= y * 2 + core
            for j, dz in enumerate(places_z):
                i = len(hidden)
                keys[pl.ds(T * i, T), :] = jnp.transpose(ref[j])
                values[:, pl.ds(T * i, T)] = ref[j, :KL, :]
                if place == (0, 0) and dz == 0:
                    diagonal = i
                hidden.append(jnp.where(dz <= z if dz else before, 0.0, NEGATIVE))
        span = T * len(hidden)

        def step(i):
            cols = pl.ds(i * COLS, COLS)
            scores = dot(keys[:span, :], q_ref[:, cols])
            blocks = [scores[T * j : T * j + T] for j in range(len(hidden))]
            if diagonal is not None:
                key = lax.broadcasted_iota(jnp.int32, (T, COLS), 0)
                token = lax.broadcasted_iota(jnp.int32, (T, COLS), 1) & (T - 1)
                blocks[diagonal] = jnp.where(key <= token, blocks[diagonal], NEGATIVE)
            highest = [
                jnp.max(block, axis=0, keepdims=True) + bias
                for block, bias in zip(blocks, hidden)
            ]
            highest = functools.reduce(jnp.maximum, highest)
            if not fresh:
                if first or number > 0:
                    m_old, l_old, acc_old = m_ref[:, cols], l_ref[:, cols], acc_ref[:, cols]
                else:
                    m_old, l_old, acc_old = m_in[:, cols], l_in[:, cols], acc_in[:, cols]
                highest = jnp.maximum(highest, m_old)
                factor = jnp.exp2(m_old - highest)
            weights = [
                jnp.exp2(block - (highest - bias)) for block, bias in zip(blocks, hidden)
            ]
            total = functools.reduce(
                jnp.add, [jnp.sum(w, axis=0, keepdims=True) for w in weights]
            )
            added = dot(
                values[:, :span], jnp.concatenate([w.astype(BF) for w in weights], axis=0)
            )
            if not fresh:
                total = total + l_old * factor
                added = added + acc_old * factor
            m_ref[:, cols] = highest
            l_ref[:, cols] = total
            acc_ref[:, cols] = added

        for i in range(ROWS // COLS):
            step(i)
    if last:
        outs = []
        for head in range(HEADS):
            cols = pl.ds(T * head, T)
            mean = (acc_ref[:, cols] / l_ref[:, cols]).astype(BF)
            outs.append(dot(up_ref[pl.ds(VDIM * head, VDIM), :], mean))
        out_ref[...] = jnp.transpose(jnp.concatenate(outs, axis=0)).astype(BF)


def attend(ep, queries, up, groups, first, last, state):
    latents = [array for group in groups for _, _, array in group]
    groups = tuple(tuple((place, dz) for place, dz, _ in group) for group in groups)
    blocks = max(sum(len(dz) for _, dz in group) for group in groups)
    carried = [
        jax.ShapeDtypeStruct((1, ROWS), F32),
        jax.ShapeDtypeStruct((1, ROWS), F32),
        jax.ShapeDtypeStruct((KL, ROWS), F32),
    ]
    args = [ep[None], queries, *latents]
    if last:
        args.append(up)
    aliases = {}
    if not first:
        if not last:
            aliases = {len(args) + i: i for i in range(3)}
        args += state
    scratch = [pltpu.VMEM((T * blocks, LAT), BF), pltpu.VMEM((KL, T * blocks), BF)]
    if last:
        out_shape = [jax.ShapeDtypeStruct((T, HEADS * VDIM), BF)]
        scratch = [pltpu.VMEM(s.shape, F32) for s in carried] + scratch
    else:
        out_shape = carried
    return pl.pallas_call(
        functools.partial(attend_kernel, groups, first, last),
        out_shape=out_shape,
        in_specs=[pl.BlockSpec(memory_space=pltpu.SMEM)] + [VMEM] * (len(args) - 1),
        out_specs=[VMEM] * len(out_shape),
        scratch_shapes=scratch,
        input_output_aliases=aliases,
        compiler_params=params(32),
        name="attend",
    )(*args)


def ring(x, shift):
    return lax.ppermute(x, "tp", [(i, (i + shift) % TP) for i in range(TP)])


def from_all(x):
    return [x] + [ring(x, shift) for shift in (1, 2, 3)]


def along_z(x, shift):
    return lax.ppermute(x, "ep", [(i, (i + 8 * shift) % EP) for i in range(EP)])


def along_y(x, shift):
    pairs = [(i, (i & ~6) | ((i + 2 * shift) & 6)) for i in range(EP)]
    return lax.ppermute(x, "ep", pairs)


def other_core(x):
    return lax.ppermute(x, "ep", [(i, i ^ 1) for i in range(EP)])


THREE = (1, 0, 7)
FIVE = (4, 3, 2, 6, 5)
EIGHT = THREE + FIVE


def slot_weights(routes, gates):
    experts = jnp.arange(EXPERTS, dtype=jnp.int32)
    onehot = (routes[:, :, None] == experts[None, None, :]).astype(F32)
    named = jnp.sum(onehot, axis=1)
    earlier = jnp.tril(jnp.ones((T, T), BF), -1)
    before = dot(earlier, named.astype(BF))
    slots = jnp.sum(before[:, None, :] * onehot, axis=2).astype(jnp.int32)
    place = routes * CAP + slots
    lane = jnp.arange(SLOTS, dtype=jnp.int32)
    weights = jnp.zeros((T, SLOTS), F32)
    for k in range(routes.shape[1]):
        weights = weights + jnp.where(place[:, k : k + 1] == lane[None], gates[:, k : k + 1], 0.0)
    return weights


def pack_kernel(hidden_ref, embed_ref, down_ref, query_ref, latent_ref, out_ref):
    hidden, embed, down, query, latent = (
        ref[...].astype(F32) for ref in (hidden_ref, embed_ref, down_ref, query_ref, latent_ref)
    )
    rows = [latent[r : r + 1] for r in range(4)]
    out_ref[pl.ds(0, 112), :] = jnp.concatenate([hidden, embed], axis=0).astype(BF)
    spare = jnp.zeros((1, 128), F32)
    group_1 = jnp.concatenate(
        [
            down[:, :F],
            jnp.concatenate([rows[0][:, 1536:1920], rows[1][:, 1536:1920], spare], axis=1),
            jnp.concatenate([rows[2][:, 1536:1920], rows[3][:, 1536:1920], spare], axis=1),
        ],
        axis=0,
    )
    out_ref[pl.ds(112, 16), :] = group_1.astype(BF)
    group_2 = jnp.concatenate([query[:, :F], latent[:, :F]], axis=0)
    out_ref[pl.ds(128, 16), :] = group_2.astype(BF)
    tail = jnp.concatenate([down[:, F:], jnp.zeros((14, 96), F32)], axis=1)
    left = jnp.concatenate(
        [
            tail,
            jnp.concatenate([rows[0][:, 1920:], rows[1][:, 1920:]], axis=1),
            jnp.concatenate([rows[2][:, 1920:], rows[3][:, 1920:]], axis=1),
        ],
        axis=0,
    )
    right = jnp.concatenate([query[:, F:], latent[:, F:1536]], axis=0)
    out_ref[pl.ds(144, 16), :] = jnp.concatenate([left, right], axis=1).astype(BF)


def split_gates_kernel(weights_ref, hi_ref, lo_ref):
    weights = weights_ref[...]
    hi = weights.astype(BF)
    hi_ref[...] = hi
    lo_ref[...] = (weights - hi.astype(F32)).astype(BF)


def shards(
    hidden_in, next_embed, expert_rows, routes, gates, gain_hidden, gain_embed, join_hidden,
    join_embed, gain_block, down_weight, gain_query, gain_latent, query_up, latent_up,
):
    ep = lax.axis_index("ep")
    tp = lax.axis_index("tp")
    order = jnp.mod(tp - jnp.arange(TP, dtype=jnp.int32), TP)
    order = jnp.concatenate([order, ep[None]])
    smem = pl.BlockSpec(memory_space=pltpu.SMEM)

    packed = lax.all_gather(
        pl.pallas_call(
            pack_kernel,
            out_shape=jax.ShapeDtypeStruct((PACK, F), BF),
            in_specs=[VMEM] * 5,
            out_specs=VMEM,
            name="pack",
        )(join_hidden, join_embed, down_weight, query_up, latent_up),
        "ep",
        axis=0,
        tiled=False,
    )
    received = lax.all_to_all(expert_rows, "ep", split_axis=1, concat_axis=0, tiled=True)
    table = received.reshape(SLOTS, F)

    embeds = from_all(
        pl.pallas_call(
            embed_kernel,
            out_shape=jax.ShapeDtypeStruct((T, 1024), BF),
            in_specs=[VMEM] * 2,
            out_specs=VMEM,
            name="embed",
        )(next_embed, gain_embed[None])
    )
    hi, lo = pl.pallas_call(
        split_gates_kernel,
        out_shape=[jax.ShapeDtypeStruct((T, SLOTS), BF)] * 2,
        in_specs=[VMEM],
        out_specs=[VMEM] * 2,
        name="split_gates",
    )(slot_weights(routes, gates))

    position = (ep * T + jnp.arange(T, dtype=jnp.int32)).astype(F32)
    freq = 10000.0 ** (-jnp.arange(ROPE // 2, dtype=F32) / (ROPE // 2))
    phase = freq[:, None] * position[None, :]
    cosine = jnp.cos(phase)
    sine = jnp.sin(phase)

    hiddens = from_all(
        pl.pallas_call(
            combine_kernel,
            out_shape=jax.ShapeDtypeStruct((T, 1024), BF),
            in_specs=[VMEM] * 5,
            out_specs=VMEM,
            compiler_params=params(32),
            name="combine",
        )(hi, lo, table, hidden_in, gain_hidden[None])
    )
    joined, part, query_part = pl.pallas_call(
        join_kernel,
        out_shape=[
            jax.ShapeDtypeStruct((T, F), BF),
            jax.ShapeDtypeStruct((T, KL + 128), BF),
            jax.ShapeDtypeStruct((T, QL), BF),
        ],
        in_specs=[smem] + [VMEM] * 9 + [HBM],
        out_specs=[VMEM] * 3,
        scratch_shapes=[
            pltpu.VMEM((EP, 64, F), BF),
            pltpu.VMEM((EP, 64, F), BF),
            pltpu.VMEM((EP, 16, F), BF),
            pltpu.VMEM((EP, 16, 256), BF),
            pltpu.SemaphoreType.DMA((3, 4)),
        ],
        compiler_params=params(50),
        name="join",
    )(order, *hiddens, *embeds, gain_block[None], packed)

    part, later = lax.optimization_barrier((part, packed))
    parts = from_all(part)
    key_up, value_up = pl.pallas_call(
        up_kernel,
        out_shape=[
            jax.ShapeDtypeStruct((KL, HEADS * 128), BF),
            jax.ShapeDtypeStruct((HEADS * VDIM, KL), BF),
        ],
        in_specs=[HBM],
        out_specs=[VMEM] * 2,
        scratch_shapes=[pltpu.VMEM((EP, 48, F), BF), pltpu.SemaphoreType.DMA],
        compiler_params=params(50),
        name="up",
    )(later)
    parts, key_up, value_up = lax.optimization_barrier((parts, key_up, value_up))
    latent, scale = pl.pallas_call(
        latent_kernel,
        out_shape=[jax.ShapeDtypeStruct((LAT, T), BF), jax.ShapeDtypeStruct((T, 128), F32)],
        in_specs=[VMEM] * 7,
        out_specs=[VMEM] * 2,
        name="latent",
    )(*parts, gain_latent[None], cosine, sine)
    three = jnp.stack([along_z(latent, 1), latent, along_z(latent, -1)])
    five = along_z(three, 3), along_z(three[:2], -3)
    three_1, three_3 = along_y(three, 1), along_y(three, -1)
    other_three = other_core(three)
    three_1, three_3, other_three, key_up = lax.optimization_barrier(
        (three_1, three_3, other_three, key_up)
    )
    queries = pl.pallas_call(
        query_kernel,
        out_shape=jax.ShapeDtypeStruct((LAT, ROWS), BF),
        in_specs=[VMEM] * 9 + [HBM],
        out_specs=VMEM,
        scratch_shapes=[pltpu.VMEM((EP, 32, F), BF), pltpu.SemaphoreType.DMA],
        compiler_params=params(50),
        name="query",
    )(*from_all(query_part), scale, gain_query[None], cosine, sine, key_up, packed)
    five, queries = lax.optimization_barrier((five, queries))
    five = jnp.concatenate(five)
    five_1, five_3 = along_y(five, 1), along_y(five, -1)
    call = functools.partial(attend, ep, queries, value_up)
    state = call(
        [
            [((0, 0), THREE, three), ((0, 0), FIVE, five)],
            [((0, 1), THREE, other_three), ((0, 1), FIVE, other_core(five))],
            [((1, 0), THREE, three_1), ((3, 0), THREE, three_3)],
        ],
        True,
        False,
        None,
    )
    three_1, three_3, five_1, five_3, state = lax.optimization_barrier(
        (three_1, three_3, five_1, five_3, state)
    )
    chunk_2 = along_y(three_1, 1), along_y(five_3, -1)
    far_1 = other_core(jnp.concatenate([three_1, five_1]))
    far_3 = other_core(jnp.concatenate([three_3, five_3]))
    state = call([[((1, 0), FIVE, five_1), ((3, 0), FIVE, five_3)]], False, False, state)
    chunk_2, state = lax.optimization_barrier((chunk_2, state))
    far_2 = other_core(jnp.concatenate(chunk_2))
    state = call([[((1, 1), EIGHT, far_1)], [((3, 1), EIGHT, far_3)]], False, False, state)
    (attended,) = call(
        [
            [((2, 0), THREE, chunk_2[0]), ((2, 0), FIVE, chunk_2[1])],
            [((2, 1), EIGHT, far_2)],
        ],
        False,
        True,
        state,
    )
    return (joined, attended)


def solution(mesh):
    placed = (
        P("ep", "tp"),
        P("ep", "tp"),
        P("ep", None, None, "tp"),
        P("ep", None),
        P("ep", None),
        P("tp"),
        P("tp"),
        P("ep", "tp"),
        P("ep", "tp"),
        P("tp"),
        P(("tp", "ep"), None),
        P(),
        P(),
        P("ep", "tp"),
        P("ep", "tp"),
    )
    return jax.shard_map(
        shards,
        mesh=mesh,
        in_specs=placed,
        out_specs=(P("ep", "tp"), P("ep", "tp")),
        check_vma=False,
    )
```

```python
import functools

import jax
import jax.numpy as jnp
from jax import lax
from jax.experimental import pallas as pl
from jax.experimental.pallas import tpu as pltpu
from jax.sharding import PartitionSpec as P

D = 3584
NOPE = 64
ROPE = 32
VDIM = 64
QL = 768
KL = 256
EPS = 1e-06
NEGATIVE = -1e30
LOG2E = 1.4426950408889634

T = 128
F = 896
HEADS = 16
EP = 64
TP = 4
CAP = 8
EXPERTS = 256
SLOTS = EXPERTS * CAP
PACK = 160
LAT = KL + ROPE
ROWS = HEADS * T
COLS = 1024

BF = jnp.bfloat16
F32 = jnp.float32
VMEM = pl.BlockSpec(memory_space=pltpu.VMEM)
HBM = pl.BlockSpec(memory_space=pltpu.HBM)
MIB = 1 << 20


def params(mib):
    return pltpu.CompilerParams(vmem_limit_bytes=mib * MIB)


def dot(a, b):
    return jnp.dot(a, b, preferred_element_type=F32)


def dot_nt(a, b):
    return lax.dot_general(a, b, (((1,), (1,)), ((), ())), preferred_element_type=F32)


def split3(s):
    hi = s.astype(BF).astype(F32)
    mid = (s - hi).astype(BF).astype(F32)
    low = (s - hi - mid).astype(BF).astype(F32)
    return hi, mid, low


def lanes_of(s, width, first):
    hi, mid, low = split3(s)
    lane = lax.broadcasted_iota(jnp.int32, (s.shape[0], width), 1)
    return jnp.where(
        lane == first,
        hi,
        jnp.where(lane == first + 1, mid, jnp.where(lane == first + 2, low, 0.0)),
    )


def spread_matrix(rows, used, width, cols, skip=0):
    row = lax.broadcasted_iota(jnp.int32, (rows, cols), 0)
    col = lax.broadcasted_iota(jnp.int32, (rows, cols), 1)
    part = (col & (width - 1)) - skip
    target = jnp.where(
        (part >= 0) & (part < used), (col >> (width.bit_length() - 1)) * used + part, -1
    )
    return jnp.where(row == target, 1.0, 0.0).astype(BF)


def features_store(out_ref, state, gain, skip):
    spread = spread_matrix(F, 56, 64, 1024, skip)
    squares = jnp.sum(state * state, axis=1, keepdims=True)
    scaled = dot((state * gain).astype(BF), spread)
    lanes = lanes_of(squares, 128, 0 if skip else 56)
    out_ref[:, :128] = (scaled[:, :128] + lanes).astype(BF)
    out_ref[:, 128:] = scaled[:, 128:].astype(BF)


def embed_kernel(embed_ref, gain_ref, out_ref):
    features_store(out_ref, embed_ref[...].astype(F32), gain_ref[...], 8)


def combine_kernel(hi_ref, lo_ref, table_ref, hidden_ref, gain_ref, out_ref):
    moe = dot(hi_ref[...], table_ref[...]) + dot(lo_ref[...], table_ref[...])
    features_store(out_ref, hidden_ref[...].astype(F32) + moe, gain_ref[...], 0)


def join_kernel(
    order_ref, h0, h1, h2, h3, e0, e1, e2, e3, gain_ref, packed_ref,
    joined_ref, latent_ref, query_ref, wh, we, wa, wc, sems,
):
    def chunk(half, first, number, target):
        rows = pl.ds(pl.multiple_of(16 * order_ref[number], 16), 16)
        return pltpu.make_async_copy(
            packed_ref.at[rows, pl.ds(first, 64), :],
            target.at[pl.ds(16 * number, 16)],
            sems.at[half, number],
        )

    copies_e = [chunk(1, 48, i, we) for i in range(TP)]
    copies_h = [chunk(0, 0, i, wh) for i in range(TP)]
    copy_a = pltpu.make_async_copy(packed_ref.at[:, pl.ds(112, 16), :], wa, sems.at[2, 0])
    copy_c = pltpu.make_async_copy(
        packed_ref.at[:, pl.ds(144, 16), pl.ds(0, 256)], wc, sems.at[2, 1]
    )
    for copy in copies_e + copies_h + [copy_a, copy_c]:
        copy.start()
    spread = spread_matrix(F, 14, 16, 1024)
    lane = lax.broadcasted_iota(jnp.int32, (T, 1024), 1) & 63

    def project(blocks, weights, copies, used):
        total = jnp.zeros((T, F), F32)
        squares = jnp.zeros((T, 1), F32)
        for i, ref in enumerate(blocks):
            block = ref[...].astype(F32)
            held = jnp.where(used[:, :128], 0.0, block[:, :128])
            squares = squares + jnp.sum(held, axis=1, keepdims=True)
            block = jnp.where(used, block, 0.0).astype(BF)
            copies[i].wait()
            weight = weights[pl.ds(16 * i, 16)].reshape(1024, F)
            total = total + dot(block, weight)
        return total * lax.rsqrt(squares / D + EPS)

    embed = project((e0, e1, e2, e3), we, copies_e, lane >= 8)
    joined = (project((h0, h1, h2, h3), wh, copies_h, lane < 56) + embed).astype(BF)
    joined_ref[...] = joined
    wide = joined.astype(F32)
    squares = jnp.sum(wide * wide, axis=1, keepdims=True)
    scaled = dot((wide * gain_ref[...]).astype(BF), spread).astype(BF)
    copy_a.wait()
    copy_c.wait()
    down = dot(scaled, wa[...].reshape(1024, F))
    query_ref[...] = down[:, :QL].astype(BF)
    latent_ref[:, :128] = down[:, QL:].astype(BF)
    tail = dot(scaled, wc[...].reshape(1024, 256))
    latent_ref[:, 128:] = (tail + lanes_of(squares, 256, 160)).astype(BF)


def rotate(x, cos_ref, sin_ref):
    first, second = x[: ROPE // 2], x[ROPE // 2 :]
    cosine, sine = cos_ref[...], sin_ref[...]
    return jnp.concatenate(
        [first * cosine - second * sine, first * sine + second * cosine], axis=0
    )


def add_parts(refs):
    a, b, c, d = (ref[...].astype(F32) for ref in refs)
    return (a + b) + (c + d)


def latent_kernel(p0, p1, p2, p3, gl_ref, cos_ref, sin_ref, latent_ref, scale_ref):
    total = add_parts((p0, p1, p2, p3))
    tail = total[:, KL:]
    lane = lax.broadcasted_iota(jnp.int32, tail.shape, 1)
    squares = jnp.sum(
        jnp.where((lane >= 32) & (lane < 35), tail, 0.0), axis=1, keepdims=True
    )
    scale = lax.rsqrt(squares / D + EPS)
    key = total[:, :KL] * scale
    key = key * lax.rsqrt(jnp.mean(key * key, axis=1, keepdims=True) + EPS)
    latent_ref[:KL, :] = jnp.transpose(key * gl_ref[...]).astype(BF)
    rope = rotate(jnp.transpose(tail * scale)[:ROPE], cos_ref, sin_ref)
    latent_ref[KL:, :] = rope.astype(BF)
    scale_ref[...] = jnp.broadcast_to(scale, (T, 128))


def up_kernel(packed_ref, key_ref, value_ref, held, sem):
    copy = pltpu.make_async_copy(packed_ref.at[:, pl.ds(112, 48), :], held, sem)
    copy.start()
    row = lax.broadcasted_iota(jnp.int32, (KL, 1024), 0)
    col = lax.broadcasted_iota(jnp.int32, (KL, 1024), 1) - (row >> 2) * 16
    row = row & 3

    def pick(target):
        return jnp.where(col == target, 1.0, 0.0).astype(BF)

    copy.wait()
    group_a = held[:, 0:16, 0:768].reshape(1024, 768)
    group_b = held[:, 16:32, :].reshape(1024, F)
    group_c = held[:, 32:48, 256:].reshape(1024, 640)
    group_d = held[:, 32:48, :256].reshape(1024, 256)
    spare = pick(12 + row)
    even = pick(jnp.where(row & 1 == 0, 14 + (row >> 1), -9999))
    odd = pick(jnp.where(row & 1 == 1, 14 + (row >> 1), -9999))
    up = jnp.concatenate(
        [
            dot(spare, group_b),
            dot(spare, group_c),
            dot(even, group_a[:, :384]) + dot(odd, group_a[:, 384:]),
            dot(even, group_d[:, :128]) + dot(odd, group_d[:, 128:]),
        ],
        axis=1,
    )
    for head in range(HEADS):
        own = up[:, 128 * head : 128 * head + 128]
        key_ref[:, pl.ds(128 * head, 128)] = own.astype(BF)
        value_ref[pl.ds(VDIM * head, VDIM), :] = jnp.transpose(own)[NOPE:, :].astype(BF)


def query_kernel(
    q0, q1, q2, q3, scale_ref, gq_ref, cos_ref, sin_ref, up_ref, packed_ref, out_ref, held, sem
):
    copy = pltpu.make_async_copy(packed_ref.at[:, pl.ds(128, 32), :], held, sem)
    copy.start()
    spread = spread_matrix(QL, 12, 16, 1024)
    query = add_parts((q0, q1, q2, q3)) * scale_ref[:, :1]
    query = query * lax.rsqrt(jnp.mean(query * query, axis=1, keepdims=True) + EPS)
    query = dot((query * gq_ref[...]).astype(BF), spread).astype(BF)
    copy.wait()
    group_b = held[:, 0:16, :].reshape(1024, F)
    group_c = held[:, 16:32, 256:].reshape(1024, 640)
    projected = jnp.transpose(
        jnp.concatenate([dot(query, group_b), dot(query, group_c)], axis=1)
    )
    scale = (NOPE + ROPE) ** (-0.5) * LOG2E
    width = NOPE + ROPE
    for head in range(HEADS):
        nope = projected[width * head : width * head + NOPE].astype(BF)
        absorbed = dot(up_ref[:, pl.ds(128 * head, NOPE)], nope)
        cols = pl.ds(T * head, T)
        out_ref[:KL, cols] = (absorbed * scale).astype(BF)
        rope = rotate(projected[width * head + NOPE : width * head + width], cos_ref, sin_ref)
        out_ref[KL:, cols] = (rope * scale).astype(BF)


def attend_kernel(groups, first, last, index_ref, q_ref, *rest):
    held = []
    for group in groups:
        held.append(rest[: len(group)])
        rest = rest[len(group) :]
    if last:
        up_ref, rest = rest[0], rest[1:]
    if not first:
        (m_in, l_in, acc_in), rest = rest[:3], rest[3:]
    if last:
        out_ref, rest = rest[0], rest[1:]
        m_ref, l_ref, acc_ref, keys, values = rest
    else:
        m_ref, l_ref, acc_ref, keys, values = rest
    ep = index_ref[0]
    z, y, core = ep >> 3, (ep >> 1) & 3, ep & 1

    for number, group in enumerate(groups):
        fresh = first and number == 0
        diagonal, hidden = None, []
        for (place, places_z), ref in zip(group, held[number]):
            dy, dc = place
            before = ((y - dy) & 3) * 2 + (core ^ dc) <= y * 2 + core
            for j, dz in enumerate(places_z):
                i = len(hidden)
                keys[pl.ds(T * i, T), :] = jnp.transpose(ref[j])
                values[:, pl.ds(T * i, T)] = ref[j, :KL, :]
                if place == (0, 0) and dz == 0:
                    diagonal = i
                hidden.append(jnp.where(dz <= z if dz else before, 0.0, NEGATIVE))
        span = T * len(hidden)

        def step(i):
            cols = pl.ds(i * COLS, COLS)
            scores = dot(keys[:span, :], q_ref[:, cols])
            blocks = [scores[T * j : T * j + T] for j in range(len(hidden))]
            if diagonal is not None:
                key = lax.broadcasted_iota(jnp.int32, (T, COLS), 0)
                token = lax.broadcasted_iota(jnp.int32, (T, COLS), 1) & (T - 1)
                blocks[diagonal] = jnp.where(key <= token, blocks[diagonal], NEGATIVE)
            highest = [
                jnp.max(block, axis=0, keepdims=True) + bias
                for block, bias in zip(blocks, hidden)
            ]
            highest = functools.reduce(jnp.maximum, highest)
            if not fresh:
                if first or number > 0:
                    m_old, l_old, acc_old = m_ref[:, cols], l_ref[:, cols], acc_ref[:, cols]
                else:
                    m_old, l_old, acc_old = m_in[:, cols], l_in[:, cols], acc_in[:, cols]
                highest = jnp.maximum(highest, m_old)
                factor = jnp.exp2(m_old - highest)
            weights = [
                jnp.exp2(block - (highest - bias)) for block, bias in zip(blocks, hidden)
            ]
            total = functools.reduce(
                jnp.add, [jnp.sum(w, axis=0, keepdims=True) for w in weights]
            )
            added = dot(
                values[:, :span], jnp.concatenate([w.astype(BF) for w in weights], axis=0)
            )
            if not fresh:
                total = total + l_old * factor
                added = added + acc_old * factor
            m_ref[:, cols] = highest
            l_ref[:, cols] = total
            acc_ref[:, cols] = added

        for i in range(ROWS // COLS):
            step(i)
    if last:
        outs = []
        for head in range(HEADS):
            cols = pl.ds(T * head, T)
            mean = (acc_ref[:, cols] / l_ref[:, cols]).astype(BF)
            outs.append(dot(up_ref[pl.ds(VDIM * head, VDIM), :], mean))
        out_ref[...] = jnp.transpose(jnp.concatenate(outs, axis=0)).astype(BF)


def attend(ep, queries, up, groups, first, last, state):
    latents = [array for group in groups for _, _, array in group]
    groups = tuple(tuple((place, dz) for place, dz, _ in group) for group in groups)
    blocks = max(sum(len(dz) for _, dz in group) for group in groups)
    carried = [
        jax.ShapeDtypeStruct((1, ROWS), F32),
        jax.ShapeDtypeStruct((1, ROWS), F32),
        jax.ShapeDtypeStruct((KL, ROWS), F32),
    ]
    args = [ep[None], queries, *latents]
    if last:
        args.append(up)
    aliases = {}
    if not first:
        if not last:
            aliases = {len(args) + i: i for i in range(3)}
        args += state
    scratch = [pltpu.VMEM((T * blocks, LAT), BF), pltpu.VMEM((KL, T * blocks), BF)]
    if last:
        out_shape = [jax.ShapeDtypeStruct((T, HEADS * VDIM), BF)]
        scratch = [pltpu.VMEM(s.shape, F32) for s in carried] + scratch
    else:
        out_shape = carried
    return pl.pallas_call(
        functools.partial(attend_kernel, groups, first, last),
        out_shape=out_shape,
        in_specs=[pl.BlockSpec(memory_space=pltpu.SMEM)] + [VMEM] * (len(args) - 1),
        out_specs=[VMEM] * len(out_shape),
        scratch_shapes=scratch,
        input_output_aliases=aliases,
        compiler_params=params(32),
        name="attend",
    )(*args)


def ring(x, shift):
    return lax.ppermute(x, "tp", [(i, (i + shift) % TP) for i in range(TP)])


def from_all(x):
    return [x] + [ring(x, shift) for shift in (1, 2, 3)]


def along_z(x, shift):
    return lax.ppermute(x, "ep", [(i, (i + 8 * shift) % EP) for i in range(EP)])


def along_y(x, shift):
    pairs = [(i, (i & ~6) | ((i + 2 * shift) & 6)) for i in range(EP)]
    return lax.ppermute(x, "ep", pairs)


def other_core(x):
    return lax.ppermute(x, "ep", [(i, i ^ 1) for i in range(EP)])


THREE = (1, 0, 7)
FIVE = (4, 3, 2, 6, 5)
EIGHT = THREE + FIVE


def slot_weights(routes, gates):
    experts = jnp.arange(EXPERTS, dtype=jnp.int32)
    onehot = (routes[:, :, None] == experts[None, None, :]).astype(F32)
    named = jnp.sum(onehot, axis=1)
    earlier = jnp.tril(jnp.ones((T, T), BF), -1)
    before = dot(earlier, named.astype(BF))
    slots = jnp.sum(before[:, None, :] * onehot, axis=2).astype(jnp.int32)
    place = routes * CAP + slots
    lane = jnp.arange(SLOTS, dtype=jnp.int32)
    weights = jnp.zeros((T, SLOTS), F32)
    for k in range(routes.shape[1]):
        weights = weights + jnp.where(place[:, k : k + 1] == lane[None], gates[:, k : k + 1], 0.0)
    return weights


def pack_kernel(hidden_ref, embed_ref, down_ref, query_ref, latent_ref, out_ref):
    hidden, embed, down, query, latent = (
        ref[...].astype(F32) for ref in (hidden_ref, embed_ref, down_ref, query_ref, latent_ref)
    )
    rows = [latent[r : r + 1] for r in range(4)]
    out_ref[pl.ds(0, 112), :] = jnp.concatenate([hidden, embed], axis=0).astype(BF)
    spare = jnp.zeros((1, 128), F32)
    group_1 = jnp.concatenate(
        [
            down[:, :F],
            jnp.concatenate([rows[0][:, 1536:1920], rows[1][:, 1536:1920], spare], axis=1),
            jnp.concatenate([rows[2][:, 1536:1920], rows[3][:, 1536:1920], spare], axis=1),
        ],
        axis=0,
    )
    out_ref[pl.ds(112, 16), :] = group_1.astype(BF)
    group_2 = jnp.concatenate([query[:, :F], latent[:, :F]], axis=0)
    out_ref[pl.ds(128, 16), :] = group_2.astype(BF)
    tail = jnp.concatenate([down[:, F:], jnp.zeros((14, 96), F32)], axis=1)
    left = jnp.concatenate(
        [
            tail,
            jnp.concatenate([rows[0][:, 1920:], rows[1][:, 1920:]], axis=1),
            jnp.concatenate([rows[2][:, 1920:], rows[3][:, 1920:]], axis=1),
        ],
        axis=0,
    )
    right = jnp.concatenate([query[:, F:], latent[:, F:1536]], axis=0)
    out_ref[pl.ds(144, 16), :] = jnp.concatenate([left, right], axis=1).astype(BF)


def split_gates_kernel(weights_ref, hi_ref, lo_ref):
    weights = weights_ref[...]
    hi = weights.astype(BF)
    hi_ref[...] = hi
    lo_ref[...] = (weights - hi.astype(F32)).astype(BF)


def shards(
    hidden_in, next_embed, expert_rows, routes, gates, gain_hidden, gain_embed, join_hidden,
    join_embed, gain_block, down_weight, gain_query, gain_latent, query_up, latent_up,
):
    ep = lax.axis_index("ep")
    tp = lax.axis_index("tp")
    order = jnp.mod(tp - jnp.arange(TP, dtype=jnp.int32), TP)
    order = jnp.concatenate([order, ep[None]])
    smem = pl.BlockSpec(memory_space=pltpu.SMEM)

    packed = lax.all_gather(
        pl.pallas_call(
            pack_kernel,
            out_shape=jax.ShapeDtypeStruct((PACK, F), BF),
            in_specs=[VMEM] * 5,
            out_specs=VMEM,
            name="pack",
        )(join_hidden, join_embed, down_weight, query_up, latent_up),
        "ep",
        axis=0,
        tiled=False,
    )
    received = lax.all_to_all(expert_rows, "ep", split_axis=1, concat_axis=0, tiled=True)
    table = received.reshape(SLOTS, F)

    embeds = from_all(
        pl.pallas_call(
            embed_kernel,
            out_shape=jax.ShapeDtypeStruct((T, 1024), BF),
            in_specs=[VMEM] * 2,
            out_specs=VMEM,
            name="embed",
        )(next_embed, gain_embed[None])
    )
    hi, lo = pl.pallas_call(
        split_gates_kernel,
        out_shape=[jax.ShapeDtypeStruct((T, SLOTS), BF)] * 2,
        in_specs=[VMEM],
        out_specs=[VMEM] * 2,
        name="split_gates",
    )(slot_weights(routes, gates))

    position = (ep * T + jnp.arange(T, dtype=jnp.int32)).astype(F32)
    freq = 10000.0 ** (-jnp.arange(ROPE // 2, dtype=F32) / (ROPE // 2))
    phase = freq[:, None] * position[None, :]
    cosine = jnp.cos(phase)
    sine = jnp.sin(phase)

    hiddens = from_all(
        pl.pallas_call(
            combine_kernel,
            out_shape=jax.ShapeDtypeStruct((T, 1024), BF),
            in_specs=[VMEM] * 5,
            out_specs=VMEM,
            compiler_params=params(32),
            name="combine",
        )(hi, lo, table, hidden_in, gain_hidden[None])
    )
    joined, part, query_part = pl.pallas_call(
        join_kernel,
        out_shape=[
            jax.ShapeDtypeStruct((T, F), BF),
            jax.ShapeDtypeStruct((T, KL + 128), BF),
            jax.ShapeDtypeStruct((T, QL), BF),
        ],
        in_specs=[smem] + [VMEM] * 9 + [HBM],
        out_specs=[VMEM] * 3,
        scratch_shapes=[
            pltpu.VMEM((EP, 64, F), BF),
            pltpu.VMEM((EP, 64, F), BF),
            pltpu.VMEM((EP, 16, F), BF),
            pltpu.VMEM((EP, 16, 256), BF),
            pltpu.SemaphoreType.DMA((3, 4)),
        ],
        compiler_params=params(50),
        name="join",
    )(order, *hiddens, *embeds, gain_block[None], packed)

    part, later = lax.optimization_barrier((part, packed))
    parts = from_all(part)
    key_up, value_up = pl.pallas_call(
        up_kernel,
        out_shape=[
            jax.ShapeDtypeStruct((KL, HEADS * 128), BF),
            jax.ShapeDtypeStruct((HEADS * VDIM, KL), BF),
        ],
        in_specs=[HBM],
        out_specs=[VMEM] * 2,
        scratch_shapes=[pltpu.VMEM((EP, 48, F), BF), pltpu.SemaphoreType.DMA],
        compiler_params=params(50),
        name="up",
    )(later)
    parts, key_up, value_up = lax.optimization_barrier((parts, key_up, value_up))
    latent, scale = pl.pallas_call(
        latent_kernel,
        out_shape=[jax.ShapeDtypeStruct((LAT, T), BF), jax.ShapeDtypeStruct((T, 128), F32)],
        in_specs=[VMEM] * 7,
        out_specs=[VMEM] * 2,
        name="latent",
    )(*parts, gain_latent[None], cosine, sine)
    three = jnp.stack([along_z(latent, 1), latent, along_z(latent, -1)])
    five = along_z(three, 3), along_z(three[:2], -3)
    query_parts = from_all(query_part)
    near, query_parts[1] = lax.optimization_barrier((three, query_parts[1]))
    three_1, three_3 = along_y(near, 1), along_y(near, -1)
    other_three = other_core(near)
    queries = pl.pallas_call(
        query_kernel,
        out_shape=jax.ShapeDtypeStruct((LAT, ROWS), BF),
        in_specs=[VMEM] * 9 + [HBM],
        out_specs=VMEM,
        scratch_shapes=[pltpu.VMEM((EP, 32, F), BF), pltpu.SemaphoreType.DMA],
        compiler_params=params(50),
        name="query",
    )(*query_parts, scale, gain_query[None], cosine, sine, key_up, packed)
    five, queries = lax.optimization_barrier((five, queries))
    five = jnp.concatenate(five)
    five_1, five_3 = along_y(five, 1), along_y(five, -1)
    call = functools.partial(attend, ep, queries, value_up)
    state = call(
        [
            [((0, 0), THREE, three), ((0, 0), FIVE, five)],
            [((0, 1), THREE, other_three), ((0, 1), FIVE, other_core(five))],
            [((1, 0), THREE, three_1), ((3, 0), THREE, three_3)],
        ],
        True,
        False,
        None,
    )
    three_1, three_3, five_1, five_3, state = lax.optimization_barrier(
        (three_1, three_3, five_1, five_3, state)
    )
    chunk_2 = along_y(three_1, 1), along_y(five_3, -1)
    far_1 = other_core(jnp.concatenate([three_1, five_1]))
    far_3 = other_core(jnp.concatenate([three_3, five_3]))
    state = call([[((1, 0), FIVE, five_1), ((3, 0), FIVE, five_3)]], False, False, state)
    chunk_2, state = lax.optimization_barrier((chunk_2, state))
    far_2 = other_core(jnp.concatenate(chunk_2))
    state = call([[((1, 1), EIGHT, far_1)], [((3, 1), EIGHT, far_3)]], False, False, state)
    (attended,) = call(
        [
            [((2, 0), THREE, chunk_2[0]), ((2, 0), FIVE, chunk_2[1])],
            [((2, 1), EIGHT, far_2)],
        ],
        False,
        True,
        state,
    )
    return (joined, attended)


def solution(mesh):
    placed = (
        P("ep", "tp"),
        P("ep", "tp"),
        P("ep", None, None, "tp"),
        P("ep", None),
        P("ep", None),
        P("tp"),
        P("tp"),
        P("ep", "tp"),
        P("ep", "tp"),
        P("tp"),
        P(("tp", "ep"), None),
        P(),
        P(),
        P("ep", "tp"),
        P("ep", "tp"),
    )
    return jax.shard_map(
        shards,
        mesh=mesh,
        in_specs=placed,
        out_specs=(P("ep", "tp"), P("ep", "tp")),
        check_vma=False,
    )
```
